512 devices in a mesh: dp: 32 (over x, y), space: 16 (over z, core).
Axes of the slice: x: 4, y: 8, z: 8, core: 2. Of those that a mesh axis runs over, the one named last changes fastest.
Arguments:
- features: bfloat16 [32, 512, 64, 256], P('dp', 'space'), may hold values from -6 to 6
- cotangent: bfloat16 [32, 256, 64, 256], P('dp', 'space'), may hold values from -6 to 6
- weights: bfloat16 [7, 256, 256], replicated, may hold values from -0.125 to 0.125
- counts: int32 [32, 16], P('dp', 'space'), may hold values from 0 to 32, as said below
- neighbours: int32 [32, 512, 6], P('dp', 'space'), may hold values from 0 to 96, as said below
- send_list: int32 [32, 16, 16, 2], P('dp', 'space'), may hold values from 0 to 32, as said below
- recv_list: int32 [32, 256], P('dp', 'space'), may hold values from 0 to 31, as said below
Outputs:
- voxel_out: bfloat16 [32, 512, 64, 256], P('dp', 'space')
- weight_grad: bfloat16 [7, 256, 256], replicated
The draws below stay inside these ranges and needn't reach their ends.
Inputs may be any that keep to these rules, and one draw needn't show every extreme that they name: The live slots of an owner are its first counts slots; the counts of one scene sum to 16 times the number of space devices, and some owner of every scene holds 32. `send_list`: entry [g, s, j, c] is the c-th (rising) live Morton slot of owner s whose block goes to balanced owner j, or 32 past the last one; every live slot appears exactly once, at most 2 from one owner to one balanced owner, and an owner holding 32 sends exactly 2 to each. `recv_list`: entry [g, j * 16 + r] is s * 2 + c, naming the block that owner s sends as its c-th to balanced owner j; the entries of one balanced owner are distinct and cover all blocks sent to it, so every balanced owner holds exactly 16 blocks. `neighbours`: entries name live slots only; slots that are not live have none in every direction; only -x names the previous owner and only +x the next one.
All inputs are finite; a program needn't handle non-finite values.
Results may differ from the reference program's by a relative error of at most 0.012.
Values may be sent and summed in bfloat16 or wider, within the bound.
A program may use at most 64 MiB of HBM per device.

```python
import math
import jax
import jax.numpy as jnp
from jax import lax

C = 256
BLOCK_VOXELS = 64
CAP = 2
SLOTS = 32
BAL = 16
N_DP = 32
N_SPACE = 16


def scene_plan(key):
    key_pairs, key_depth, key_recv, key_order, key_links = jax.random.split(key, 5)
    shuffled = jax.random.permutation(key_pairs, N_SPACE)
    depth_shift = jax.random.randint(key_depth, (N_SPACE // 2,), 0, BAL + 1)
    depth_shift = depth_shift.at[0].set(BAL)
    paired = jnp.stack([BAL + depth_shift, BAL - depth_shift], 1).reshape(N_SPACE).astype(jnp.int32)
    counts = jnp.zeros((N_SPACE,), jnp.int32).at[shuffled].set(paired)
    offsets = jnp.cumsum(counts) - counts
    receivers = jax.random.permutation(key_recv, N_SPACE)
    residue = jnp.arange(N_SPACE, dtype=jnp.int32)
    places = jnp.arange(CAP, dtype=jnp.int32)
    first_block = (residue[None, :] - offsets[:, None]) % N_SPACE
    block_index = first_block[:, :, None] + places[None, None, :] * N_SPACE
    block_index = jnp.where(block_index < counts[:, None, None], block_index, SLOTS).astype(jnp.int32)
    send_table = jnp.zeros((N_SPACE, N_SPACE, CAP), jnp.int32).at[:, receivers, :].set(block_index)
    flat_index = jnp.arange(N_SPACE * CAP, dtype=jnp.int32)

    def receiver_list(column, order_key):
        filled = column.reshape(-1) < SLOTS
        ranking = jnp.where(filled, flat_index, flat_index + N_SPACE * CAP)
        ordered = jnp.argsort(ranking)[:BAL].astype(jnp.int32)
        return ordered[jax.random.permutation(order_key, BAL)]
    recv_table = jax.vmap(receiver_list)(jnp.transpose(send_table, (1, 0, 2)), jax.random.split(key_order, N_SPACE))
    left_counts = jnp.concatenate([jnp.zeros((1,), jnp.int32), counts[:-1]])
    right_counts = jnp.concatenate([counts[1:], jnp.zeros((1,), jnp.int32)])
    key_have, key_remote, key_pick = jax.random.split(key_links, 3)
    present = jax.random.randint(key_have, (N_SPACE, SLOTS, 6), 0, 2)
    remote = jax.random.randint(key_remote, (N_SPACE, SLOTS, 6), 0, 2)
    picked = jax.random.randint(key_pick, (N_SPACE, SLOTS, 6), 0, 1 << 20)
    slot_ids = jnp.arange(SLOTS, dtype=jnp.int32)[None, :, None]
    local_choice = picked % jnp.maximum(counts, 1)[:, None, None]
    local_ok = (present == 1) & (local_choice != slot_ids)
    direction = jnp.arange(6, dtype=jnp.int32)[None, None, :]
    side_count = jnp.where(direction == 0, left_counts[:, None, None], jnp.where(direction == 1, right_counts[:, None, None], 0))
    side_base = jnp.where(direction == 0, SLOTS, 2 * SLOTS)
    remote_ok = (present == 1) & (remote == 1) & (side_count > 0)
    remote_choice = side_base + picked % jnp.maximum(side_count, 1)
    link_index = jnp.where(remote_ok, remote_choice, jnp.where(local_ok, local_choice, 3 * SLOTS))
    live_slot = slot_ids < counts[:, None, None]
    link_index = jnp.where(live_slot, link_index, 3 * SLOTS).astype(jnp.int32)
    return (counts, send_table, recv_table, link_index)


def full_plan(key):
    return jax.vmap(scene_plan)(jax.random.split(key, N_DP))


def draw_counts(key, part):
    return full_plan(key)[0]


def draw_send_list(key, part):
    return full_plan(key)[1]


def draw_recv_list(key, part):
    return full_plan(key)[2].reshape(N_DP, N_SPACE * BAL)


def draw_neighbours(key, part):
    return full_plan(key)[3].reshape(N_DP, N_SPACE * SLOTS, 6)


def block_levels(key, extent, shards, smallest, largest):
    def one(dim, shards_of):
        steps = jax.random.uniform(jax.random.fold_in(jax.random.fold_in(key, 6), dim), (shards_of,), jnp.float32, smallest / len(shards), largest / len(shards))
        return jnp.repeat(jnp.exp(steps), extent[dim] // shards_of).reshape((-1,) + (1,) * (len(extent) - dim - 1))

    factor_of = one(*shards[0])
    for cut in shards[1:]:
        factor_of = factor_of * one(*cut)
    return factor_of


def centred(rng, shape, width, reach, cuts=(), kind=jnp.bfloat16):
    result = jax.random.normal(rng, shape, jnp.float32) * width
    if len(cuts) > 0:
        result = block_levels(rng, shape, cuts, -0.22, 0.18) * result
    return jnp.clip(result, min=-reach, max=reach).astype(kind)


def setup_inputs(seed: int = 0) -> dict:
    arg_keys = jax.random.split(jax.random.key(seed), 8)
    features = centred(arg_keys[0], (N_DP, N_SPACE * SLOTS, BLOCK_VOXELS, C), 1.0, 6.0, ((0, 32), (1, 16)))
    cotangent = centred(arg_keys[1], (N_DP, N_SPACE * BAL, BLOCK_VOXELS, C), 1.0, 6.0, ((0, 32), (1, 16)))
    weights = centred(arg_keys[2], (7, C, C), (7 * C) ** -0.5, 0.125)
    counts = draw_counts(jax.random.fold_in(arg_keys[7], 71), 0)
    neighbours = draw_neighbours(jax.random.fold_in(arg_keys[7], 71), 0)
    send_list = draw_send_list(jax.random.fold_in(arg_keys[7], 71), 0)
    recv_list = draw_recv_list(jax.random.fold_in(arg_keys[7], 71), 0)
    return dict(features=features, cotangent=cotangent, weights=weights, counts=counts, neighbours=neighbours, send_list=send_list, recv_list=recv_list)


def plane_views(blocks):
    return [blocks[:, 3], blocks[:, 0], blocks[:, :, 3], blocks[:, :, 0], blocks[:, :, :, 3], blocks[:, :, :, 0]]

def shifted_taps(blocks, faces):
    channels = blocks.shape[-1]
    tap_list = [blocks, jnp.concatenate([faces[0][:, None], blocks[:, :3]], 1), jnp.concatenate([blocks[:, 1:], faces[1][:, None]], 1), jnp.concatenate([faces[2][:, :, None], blocks[:, :, :3]], 2), jnp.concatenate([blocks[:, :, 1:], faces[3][:, :, None]], 2), jnp.concatenate([faces[4][:, :, :, None], blocks[:, :, :, :3]], 3), jnp.concatenate([blocks[:, :, :, 1:], faces[5][:, :, :, None]], 3)]
    return jnp.stack(tap_list, 0).reshape(7, -1, channels)

def reference(features, cotangent, weights, counts, neighbours, send_list, recv_list):
    channels = features.shape[-1]
    weights_wide = weights.astype(jnp.float32)

    def device_faces(local_blocks, from_left, from_right, link_rows):
        planes = plane_views(local_blocks)
        zero_face = jnp.zeros((1, 16, channels), local_blocks.dtype)
        gathered = []
        for direction in range(6):
            lookup = jnp.concatenate([planes[direction].reshape(SLOTS, 16, channels), from_left, from_right, zero_face], 0)
            gathered.append(lookup[link_rows[:, direction]].reshape(SLOTS, 4, 4, channels))
        return gathered

    def scene_step(grad_sum, inputs):
        scene_features, scene_cot, scene_counts, scene_links, scene_send, scene_recv = inputs
        blocks = scene_features.reshape(N_SPACE, SLOTS, 4, 4, 4, channels)
        lowest = blocks[:, :, 0].reshape(N_SPACE, SLOTS, 16, channels)
        highest = blocks[:, :, 3].reshape(N_SPACE, SLOTS, 16, channels)
        zero_rim = jnp.zeros((1, SLOTS, 16, channels), blocks.dtype)
        from_left = jnp.concatenate([zero_rim, highest[:-1]], 0)
        from_right = jnp.concatenate([lowest[1:], zero_rim], 0)
        faces = jax.vmap(device_faces)(blocks, from_left, from_right, scene_links.reshape(N_SPACE, SLOTS, 6))
        flat_faces = [face_block.reshape(N_SPACE * SLOTS, 4, 4, channels) for face_block in faces]
        tap_rows = shifted_taps(blocks.reshape(N_SPACE * SLOTS, 4, 4, 4, channels), flat_faces).astype(jnp.float32)
        live_slots = (jnp.arange(SLOTS, dtype=jnp.int32)[None, :] < scene_counts[:, None]).reshape(N_SPACE * SLOTS)
        live_rows = jnp.repeat(live_slots, BLOCK_VOXELS)[:, None]
        conv_out = jnp.einsum('krc,kcd->rd', tap_rows, weights_wide)
        voxel_out = jnp.where(live_rows, conv_out, 0.0).astype(jnp.bfloat16)
        positions = scene_recv.reshape(N_SPACE, BAL).astype(jnp.int32)
        source = positions // CAP
        place_index = positions % CAP
        receiver = jnp.broadcast_to(jnp.arange(N_SPACE, dtype=jnp.int32)[:, None], positions.shape)
        morton = (source * SLOTS + scene_send[source, receiver, place_index]).astype(jnp.int32)
        owned = jnp.zeros((N_SPACE * SLOTS, BLOCK_VOXELS, channels), jnp.float32)
        owned = owned.at[morton.reshape(-1)].set(scene_cot.reshape(N_SPACE * BAL, BLOCK_VOXELS, channels).astype(jnp.float32))
        grad_sum = grad_sum + jnp.einsum('krc,rd->kcd', tap_rows, owned.reshape(-1, channels))
        return (grad_sum, voxel_out.reshape(N_SPACE * SLOTS, BLOCK_VOXELS, channels))
    start_sum = jnp.zeros((7, channels, channels), jnp.float32)
    grad_sum, voxel_out = lax.scan(scene_step, start_sum, (features, cotangent, counts, neighbours, send_list, recv_list))
    grad_scale = 1.0 / math.sqrt(N_DP * N_SPACE * BAL * BLOCK_VOXELS)
    weight_grad = (grad_sum * grad_scale).astype(jnp.bfloat16)
    return (voxel_out, weight_grad)
```

```python
import functools
import math

import jax
import jax.numpy as jnp
from jax import lax
from jax.experimental import pallas as pl
from jax.experimental.pallas import tpu as pltpu
from jax.sharding import PartitionSpec as P

MESH = pl.DeviceIdType.MESH
BV = 64
LANES = 128
PARTS = 2
F32 = jnp.float32
BF16 = jnp.bfloat16


def kernel(
    dims,
    cot_hbm, feat_hbm, w_hbm, counts_s, nbr_s, send_s, recv_s,
    out_hbm, wg_hbm,
    cot, feat, w, ext_m, ext_p, taps, taps_t, vout,
    outbuf, inbuf, acc,
    core_out, core_in, x_out, x_in, gx, y_out, y_in, zbuf, ybuf, cbuf,
    local_sem, halo_ss, halo_rs, cot_ss, cot_rs,
    core_ss, core_rs, x_ss, x_rs, y_ss, y_rs, z_ss, z_rs,
    yg_ss, yg_rs, xg_ss, xg_rs, cg_ss, cg_rs,
):
    nx, ny, nz, slots, bal, channels, scale = dims
    ns = 2 * nz
    taps_w = 7 * channels
    half = taps_w // 2
    xr = half // nx
    yr = gx.shape[0] // ny
    dp = lax.axis_index("dp")
    me = lax.axis_index("space")
    x, y = dp // ny, dp % ny
    z, core = me // 2, me % 2

    def remote(src, dst, ss, rs, dev):
        return pltpu.make_async_remote_copy(
            src_ref=src, dst_ref=dst, send_sem=ss, recv_sem=rs, device_id=dev, device_id_type=MESH
        )

    def space_peer(s):
        return (dp, s)

    def x_peer(d):
        return (lax.rem(x + d, nx) * ny + y, me)

    def y_peer(d):
        return (x * ny + lax.rem(y + d, ny), me)

    def z_peer(d):
        return (dp, lax.rem(z + d, nz) * 2 + core)

    sibling = (dp, z * 2 + (1 - core))

    barrier = pltpu.get_barrier_semaphore()

    @pl.loop(1, ns)
    def _(i):
        pl.semaphore_signal(barrier, inc=1, device_id=space_peer(lax.rem(me + i, ns)), device_id_type=MESH)

    @pl.loop(1, nx)
    def _(i):
        pl.semaphore_signal(barrier, inc=1, device_id=x_peer(i), device_id_type=MESH)

    @pl.loop(1, ny)
    def _(i):
        pl.semaphore_signal(barrier, inc=1, device_id=y_peer(i), device_id_type=MESH)

    load_cot = pltpu.make_async_copy(cot_hbm, cot, local_sem.at[0])
    load_feat = pltpu.make_async_copy(feat_hbm, feat.at[pl.ds(0, slots)], local_sem.at[1])
    load_w = pltpu.make_async_copy(w_hbm, w, local_sem.at[2])
    load_cot.start()
    load_feat.start()
    load_w.start()

    def offset(i):
        k = (i + 1) // 2
        return lax.rem(nz // 2 + k * (1 - 2 * lax.rem(i, 2)) + nz, nz)

    last = nz - 1

    feat[slots] = jnp.zeros((BV, channels), BF16)
    taps[slots] = jnp.zeros((BV, taps_w), BF16)
    ext_m[2 * slots] = jnp.zeros((16, channels), BF16)
    ext_p[2 * slots] = jnp.zeros((16, channels), BF16)

    load_cot.wait()

    @pl.loop(0, ns)
    def _(t):
        i, c = t // 2, lax.rem(t, 2)
        dest = lax.rem(z - offset(i) + nz, nz) * 2 + c
        for place in range(2):
            wanted = dest * 2 + place
            pos = jnp.int32(0)
            for r in range(bal):
                pos = jnp.where(recv_s[0, r] == wanted, r, pos)
            block = cot[pos]
            for h in range(PARTS):
                outbuf[h, i, c, pl.ds(place * BV, BV), :] = block[:, h * LANES : (h + 1) * LANES]

    load_feat.wait()

    @pl.loop(0, slots)
    def _(b):
        ext_m[b] = feat[b, 48:64, :]
        ext_p[b] = feat[b, 0:16, :]

    pl.semaphore_wait(barrier, ns - 1 + nx - 1 + ny - 1)

    halo_right = remote(
        ext_m.at[pl.ds(0, slots)], ext_m.at[pl.ds(slots, slots)], halo_ss.at[0], halo_rs.at[0],
        space_peer(lax.rem(me + 1, ns)),
    )
    halo_left = remote(
        ext_p.at[pl.ds(0, slots)], ext_p.at[pl.ds(slots, slots)], halo_ss.at[1], halo_rs.at[1],
        space_peer(lax.rem(me + ns - 1, ns)),
    )
    halo_right.start()
    halo_left.start()

    def cot_copy(h, i, c):
        dest = lax.rem(z - offset(i) + nz, nz) * 2 + c
        return remote(outbuf.at[h, i, c], inbuf.at[h, i, core], cot_ss.at[h, i, c], cot_rs.at[h, i, core], space_peer(dest))

    def cot_arrival(h, i, e):
        return remote(outbuf.at[h, i, e], inbuf.at[h, i, e], cot_ss.at[h, i, e], cot_rs.at[h, i, e], sibling)

    def is_own(i, c):
        return (i == last) & (c == core)

    for h in range(PARTS):
        @pl.loop(0, ns)
        def _(t):
            i, c = t // 2, lax.rem(t, 2)

            @pl.when(jnp.logical_not(is_own(i, c)))
            def _():
                cot_copy(h, i, c).start()

        inbuf[h, last, core] = outbuf[h, last, core]

    row = lax.broadcasted_iota(jnp.int32, (BV, channels), 0)
    by = lax.rem(row // 4, 4)
    bz = lax.rem(row, 4)
    keep = (by > 0, by < 3, bz > 0, bz < 3)
    own_shift = (4, 60, 1, 63)
    side_shift = (52, 12, 61, 3)

    @pl.loop(0, slots)
    def _(b):
        blk = feat[b]
        wide = blk.astype(F32)
        taps[b, :, 0:channels] = blk
        taps[b, 16:64, channels : 2 * channels] = blk[0:48]
        taps[b, 0:48, 2 * channels : 3 * channels] = blk[16:64]
        for k in range(4):
            n = jnp.minimum(nbr_s[0, b, 2 + k], slots)
            side = feat[n].astype(F32)
            tap = jnp.where(
                keep[k], pltpu.roll(wide, own_shift[k], 0), pltpu.roll(side, side_shift[k], 0)
            )
            taps[b, :, (3 + k) * channels : (4 + k) * channels] = tap.astype(BF16)

    halo_right.wait_recv()
    halo_left.wait_recv()

    @pl.loop(0, slots)
    def _(b):
        nm = jnp.minimum(nbr_s[0, b, 0], 2 * slots)
        np_ = nbr_s[0, b, 1]
        np_ = jnp.where(np_ < slots, np_, jnp.minimum(jnp.maximum(np_ - slots, slots), 2 * slots))
        taps[b, 0:16, channels : 2 * channels] = ext_m[nm]
        taps[b, 48:64, 2 * channels : 3 * channels] = ext_p[np_]

    @pl.loop(0, nz)
    def _(i):
        zs = lax.rem(z + offset(i), nz)
        for e in range(2):
            s = zs * 2 + e
            for k in range(7):
                cols = slice(k * channels, (k + 1) * channels)
                pair = jnp.concatenate(
                    [taps[send_s[0, 0, s, 0], :, cols], taps[send_s[0, 0, s, 1], :, cols]], 0
                )
                taps_t[i, cols, e * LANES : (e + 1) * LANES] = pair.T

    load_w.wait()
    live = counts_s[0, 0] * BV

    @pl.loop(0, slots // 4)
    def _(t):
        rows = taps[pl.ds(t * 4, 4)].reshape(4 * BV, taps_w)
        conv = jnp.dot(rows, w[...], preferred_element_type=F32)
        index = lax.broadcasted_iota(jnp.int32, (4 * BV, channels), 0) + t * (4 * BV)
        conv = jnp.where(index < live, conv, 0.0)
        vout[pl.ds(t * 4, 4)] = conv.astype(BF16).reshape(4, BV, channels)

    store_out = pltpu.make_async_copy(vout, out_hbm, local_sem.at[3])
    store_out.start()

    def grad_chunk(h, i):
        for e in range(2):
            if i == last:
                @pl.when(e != core)
                def _():
                    cot_arrival(h, i, e).wait_recv()
            else:
                cot_arrival(h, i, e).wait_recv()

        @pl.loop(0, 7)
        def _(m):
            rows = pl.ds(pl.multiple_of(m * channels, channels), channels)
            term = jnp.dot(
                taps_t[i, rows, :], inbuf[h, i].reshape(2 * LANES, LANES), preferred_element_type=F32
            )
            if i == 0:
                acc[h, rows, :] = term
            else:
                acc[h, rows, :] += term

    def half_rows(c):
        return pl.ds(pl.multiple_of(c * half, 16), half)

    def core_copy(h):
        return remote(core_out.at[h], core_in.at[h], core_ss.at[h], core_rs.at[h], sibling)

    def x_copy(h, d):
        return remote(x_out.at[h, d], x_in.at[h, d], x_ss.at[h, d], x_rs.at[h, d], x_peer(d))

    def y_copy(h, d):
        return remote(y_out.at[h, d], y_in.at[h, d], y_ss.at[h, d], y_rs.at[h, d], y_peer(d))

    def z_copy(h, d):
        return remote(zbuf.at[h, z], zbuf.at[h, z], z_ss.at[h, d], z_rs.at[h, d], z_peer(d))

    def z_arrival(h, d):
        zs = lax.rem(z - d + nz, nz)
        return remote(zbuf.at[h, zs], zbuf.at[h, zs], z_ss.at[h, d], z_rs.at[h, d], z_peer(d))

    def y_rows(v):
        return pl.ds(pl.multiple_of(v * yr, 16), yr)

    def yg_copy(h, d):
        mine = ybuf.at[h, y_rows(y)]
        return remote(mine, mine, yg_ss.at[h, d], yg_rs.at[h, d], y_peer(d))

    def yg_arrival(h, d):
        theirs = ybuf.at[h, y_rows(lax.rem(y - d + ny, ny))]
        return remote(theirs, theirs, yg_ss.at[h, d], yg_rs.at[h, d], y_peer(d))

    def x_rows(v):
        return pl.ds(pl.multiple_of(core * half + v * xr, 16), xr)

    def xg_copy(h, d):
        mine = cbuf.at[h, x_rows(x)]
        return remote(mine, mine, xg_ss.at[h, d], xg_rs.at[h, d], x_peer(d))

    def xg_arrival(h, d):
        theirs = cbuf.at[h, x_rows(lax.rem(x - d + nx, nx))]
        return remote(theirs, theirs, xg_ss.at[h, d], xg_rs.at[h, d], x_peer(d))

    def cg_copy(h):
        mine = cbuf.at[h, half_rows(core)]
        return remote(mine, mine, cg_ss.at[h], cg_rs.at[h], sibling)

    def cg_arrival(h):
        theirs = cbuf.at[h, half_rows(1 - core)]
        return remote(theirs, theirs, cg_ss.at[h], cg_rs.at[h], sibling)

    def store_wg(h):
        return pltpu.make_async_copy(
            cbuf.at[h], wg_hbm.at[:, pl.ds(h * LANES, LANES)], local_sem.at[4 + h]
        )

    def sum_core(h):
        core_out[h] = acc[h, half_rows(1 - core), :].astype(BF16)
        core_copy(h).start()

    def sum_x(h):
        core_copy(h).wait_recv()
        acc[h, half_rows(core), :] += core_in[h].astype(F32)
        for d in range(1, nx):
            x_out[h, d] = acc[h, x_rows(lax.rem(x + d, nx)), :].astype(BF16)
            x_copy(h, d).start()

    def sum_y(h):
        total = acc[h, x_rows(x), :]
        for d in range(1, nx):
            x_copy(h, d).wait_recv()
            total += x_in[h, d].astype(F32)
        gx[0:xr, :] = total
        if xr < ny * yr:
            gx[xr : ny * yr, :] = jnp.zeros((ny * yr - xr, LANES), F32)
        for d in range(1, ny):
            y_out[h, d] = gx[y_rows(lax.rem(y + d, ny)), :].astype(BF16)
            y_copy(h, d).start()

    def sum_z(h):
        total = gx[y_rows(y), :]
        for d in range(1, ny):
            y_copy(h, d).wait_recv()
            total += y_in[h, d].astype(F32)
        zbuf[h, z] = total.astype(BF16)
        for d in range(1, nz):
            z_copy(h, d).start()

    def spread_y(h):
        for d in range(1, nz):
            z_arrival(h, d).wait_recv()
        total = zbuf[h, 0].astype(F32)
        for v in range(1, nz):
            total += zbuf[h, v].astype(F32)
        ybuf[h, y_rows(y), :] = (total * scale).astype(BF16)
        for d in range(1, ny):
            yg_copy(h, d).start()

    def spread_x(h):
        for d in range(1, ny):
            yg_arrival(h, d).wait_recv()
        cbuf[h, x_rows(x), :] = ybuf[h, 0:xr, :]
        for d in range(1, nx):
            xg_copy(h, d).start()

    def spread_core(h):
        for d in range(1, nx):
            xg_arrival(h, d).wait_recv()
        cg_copy(h).start()

    def finish(h):
        cg_arrival(h).wait_recv()
        store_wg(h).start()

    steps = (sum_core, sum_x, sum_y, sum_z, spread_y, spread_x, spread_core, finish)
    for i in range(nz):
        grad_chunk(0, i)
    sum_core(0)
    taken = 1
    for i in range(nz):
        grad_chunk(1, i)
        if i < nz - 1 and taken < len(steps):
            steps[taken](0)
            taken += 1
    sum_core(1)
    for step in steps[taken:]:
        step(0)
    for step in steps[1:]:
        step(1)

    halo_right.wait_send()
    halo_left.wait_send()
    for h in range(PARTS):
        @pl.loop(0, ns)
        def _(t):
            i, c = t // 2, lax.rem(t, 2)

            @pl.when(jnp.logical_not(is_own(i, c)))
            def _():
                cot_copy(h, i, c).wait_send()

        core_copy(h).wait_send()
        cg_copy(h).wait_send()
        for d in range(1, nx):
            x_copy(h, d).wait_send()
            xg_copy(h, d).wait_send()
        for d in range(1, ny):
            y_copy(h, d).wait_send()
            yg_copy(h, d).wait_send()
        for d in range(1, nz):
            z_copy(h, d).wait_send()
        store_wg(h).wait()
    store_out.wait()


def shards(dp_size, space_size, features, cotangent, weights, counts, neighbours, send_list, recv_list):
    slots, channels = features.shape[1], features.shape[-1]
    bal = cotangent.shape[1]
    ny = 1 << (dp_size.bit_length() // 2)
    nx = dp_size // ny
    nz = space_size // 2
    taps_w = 7 * channels
    half = taps_w // 2
    xr = half // nx
    yr = -(-xr // (16 * ny)) * 16
    scale = 1.0 / math.sqrt(dp_size * space_size * bal * BV)
    dma = pltpu.SemaphoreType.DMA
    vmem = pltpu.VMEM
    smem_spec = pl.BlockSpec(memory_space=pltpu.SMEM)
    any_spec = pl.BlockSpec(memory_space=pl.ANY)
    macs = 2 * slots * BV * taps_w * channels
    voxel_out, weight_grad = pl.pallas_call(
        functools.partial(kernel, (nx, ny, nz, slots, bal, channels, scale)),
        out_shape=(
            jax.ShapeDtypeStruct((slots, BV, channels), BF16),
            jax.ShapeDtypeStruct((taps_w, channels), BF16),
        ),
        in_specs=[any_spec] * 3 + [smem_spec] * 4,
        out_specs=(any_spec, any_spec),
        scratch_shapes=[
            vmem((bal, BV, channels), BF16),
            vmem((slots + 1, BV, channels), BF16),
            vmem((taps_w, channels), BF16),
            vmem((2 * slots + 1, 16, channels), BF16),
            vmem((2 * slots + 1, 16, channels), BF16),
            vmem((slots + 1, BV, taps_w), BF16),
            vmem((nz, taps_w, 2 * LANES), BF16),
            vmem((slots, BV, channels), BF16),
            vmem((PARTS, nz, 2, 2 * BV, LANES), BF16),
            vmem((PARTS, nz, 2, 2 * BV, LANES), BF16),
            vmem((PARTS, taps_w, LANES), F32),
            vmem((PARTS, half, LANES), BF16),
            vmem((PARTS, half, LANES), BF16),
            vmem((PARTS, nx, xr, LANES), BF16),
            vmem((PARTS, nx, xr, LANES), BF16),
            vmem((ny * yr, LANES), F32),
            vmem((PARTS, ny, yr, LANES), BF16),
            vmem((PARTS, ny, yr, LANES), BF16),
            vmem((PARTS, nz, yr, LANES), BF16),
            vmem((PARTS, ny * yr, LANES), BF16),
            vmem((PARTS, taps_w, LANES), BF16),
            dma((4 + PARTS,)),
            dma((2,)),
            dma((2,)),
            dma((PARTS, nz, 2)),
            dma((PARTS, nz, 2)),
            dma((PARTS,)),
            dma((PARTS,)),
            dma((PARTS, nx)),
            dma((PARTS, nx)),
            dma((PARTS, ny)),
            dma((PARTS, ny)),
            dma((PARTS, nz)),
            dma((PARTS, nz)),
            dma((PARTS, ny)),
            dma((PARTS, ny)),
            dma((PARTS, nx)),
            dma((PARTS, nx)),
            dma((PARTS,)),
            dma((PARTS,)),
        ],
        compiler_params=pltpu.CompilerParams(
            collective_id=0, has_side_effects=True, vmem_limit_bytes=48 * 1024 * 1024
        ),
        cost_estimate=pl.CostEstimate(flops=4 * macs, bytes_accessed=6 << 20, transcendentals=0),
    )(
        cotangent[0], features[0], weights.reshape(taps_w, channels),
        counts, neighbours, send_list, recv_list,
    )
    return voxel_out[None], weight_grad.reshape(7, channels, channels)


def solution(mesh):
    placed = (
        P("dp", "space", None, None),
        P("dp", "space", None, None),
        P(),
        P("dp", "space"),
        P("dp", "space", None),
        P("dp", "space", None, None),
        P("dp", "space"),
    )
    return jax.shard_map(
        functools.partial(shards, mesh.shape["dp"], mesh.shape["space"]),
        mesh=mesh,
        in_specs=placed,
        out_specs=(P("dp", "space", None, None), P()),
        check_vma=False,
    )
```

```python
import functools
import math

import jax
import jax.numpy as jnp
from jax import lax
from jax.experimental import pallas as pl
from jax.experimental.pallas import tpu as pltpu
from jax.sharding import PartitionSpec as P

MESH = pl.DeviceIdType.MESH
BV = 64
LANES = 128
PARTS = 2
F32 = jnp.float32
BF16 = jnp.bfloat16


def kernel(
    dims,
    cot_hbm, feat_hbm, w_hbm, counts_s, nbr_hbm, send_hbm, recv_hbm,
    out_hbm, wg_hbm,
    nbr_s, send_s, recv_s,
    cot, feat, w, ext_m, ext_p, taps, taps_t, vout,
    outbuf, inbuf, acc,
    core_out, core_in, x_out, x_in, gx, y_out, y_in, zbuf, ybuf, cbuf,
    local_sem, halo_ss, halo_rs, cot_ss, cot_rs,
    core_ss, core_rs, x_ss, x_rs, y_ss, y_rs, z_ss, z_rs,
    yg_ss, yg_rs, xg_ss, xg_rs, cg_ss, cg_rs,
):
    nx, ny, nz, slots, bal, channels, scale = dims
    ns = 2 * nz
    taps_w = 7 * channels
    half = taps_w // 2
    xr = half // nx
    yr = gx.shape[1] // ny
    dp = lax.axis_index("dp")
    me = lax.axis_index("space")
    x, y = dp // ny, dp % ny
    z, core = me // 2, me % 2

    def remote(src, dst, ss, rs, dev):
        return pltpu.make_async_remote_copy(
            src_ref=src, dst_ref=dst, send_sem=ss, recv_sem=rs, device_id=dev, device_id_type=MESH
        )

    def space_peer(s):
        return (dp, s)

    def x_peer(d):
        return (lax.rem(x + d, nx) * ny + y, me)

    def y_peer(d):
        return (x * ny + lax.rem(y + d, ny), me)

    def z_peer(d):
        return (dp, lax.rem(z + d, nz) * 2 + core)

    sibling = (dp, z * 2 + (1 - core))

    barrier = pltpu.get_barrier_semaphore()

    @pl.loop(1, ns)
    def _(i):
        pl.semaphore_signal(barrier, inc=1, device_id=space_peer(lax.rem(me + i, ns)), device_id_type=MESH)

    @pl.loop(1, nx)
    def _(i):
        pl.semaphore_signal(barrier, inc=1, device_id=x_peer(i), device_id_type=MESH)

    @pl.loop(1, ny)
    def _(i):
        pl.semaphore_signal(barrier, inc=1, device_id=y_peer(i), device_id_type=MESH)

    load_cot = pltpu.make_async_copy(cot_hbm, cot, local_sem.at[0])
    load_feat = pltpu.make_async_copy(feat_hbm, feat.at[pl.ds(0, slots)], local_sem.at[1])
    load_w = pltpu.make_async_copy(w_hbm, w, local_sem.at[2])
    small = [
        pltpu.make_async_copy(src, dst, local_sem.at[4 + PARTS + i])
        for i, (src, dst) in enumerate(
            ((recv_hbm, recv_s), (nbr_hbm, nbr_s), (send_hbm, send_s))
        )
    ]
    for copy in small:
        copy.start()
    load_cot.start()
    load_feat.start()
    load_w.start()

    def offset(i):
        k = (i + 1) // 2
        return lax.rem(nz // 2 + k * (1 - 2 * lax.rem(i, 2)) + nz, nz)

    last = nz - 1

    feat[slots] = jnp.zeros((BV, channels), BF16)
    taps[slots] = jnp.zeros((BV, taps_w), BF16)
    ext_m[2 * slots] = jnp.zeros((16, channels), BF16)
    ext_p[2 * slots] = jnp.zeros((16, channels), BF16)

    for copy in small:
        copy.wait()
    load_cot.wait()

    @pl.loop(0, ns)
    def _(t):
        i, c = t // 2, lax.rem(t, 2)
        dest = lax.rem(z - offset(i) + nz, nz) * 2 + c
        for place in range(2):
            wanted = dest * 2 + place
            pos = jnp.int32(0)
            for r in range(bal):
                pos = jnp.where(recv_s[0, r] == wanted, r, pos)
            block = cot[pos]
            for h in range(PARTS):
                outbuf[h, i, c, pl.ds(place * BV, BV), :] = block[:, h * LANES : (h + 1) * LANES]

    load_feat.wait()

    @pl.loop(0, slots)
    def _(b):
        ext_m[b] = feat[b, 48:64, :]
        ext_p[b] = feat[b, 0:16, :]

    pl.semaphore_wait(barrier, ns - 1 + nx - 1 + ny - 1)

    halo_right = remote(
        ext_m.at[pl.ds(0, slots)], ext_m.at[pl.ds(slots, slots)], halo_ss.at[0], halo_rs.at[0],
        space_peer(lax.rem(me + 1, ns)),
    )
    halo_left = remote(
        ext_p.at[pl.ds(0, slots)], ext_p.at[pl.ds(slots, slots)], halo_ss.at[1], halo_rs.at[1],
        space_peer(lax.rem(me + ns - 1, ns)),
    )
    halo_right.start()
    halo_left.start()

    def cot_copy(h, i, c):
        dest = lax.rem(z - offset(i) + nz, nz) * 2 + c
        return remote(outbuf.at[h, i, c], inbuf.at[h, i, core], cot_ss.at[h, i, c], cot_rs.at[h, i, core], space_peer(dest))

    def cot_arrival(h, i, e):
        return remote(outbuf.at[h, i, e], inbuf.at[h, i, e], cot_ss.at[h, i, e], cot_rs.at[h, i, e], sibling)

    def is_own(i, c):
        return (i == last) & (c == core)

    for h in range(PARTS):
        @pl.loop(0, ns)
        def _(t):
            i, c = t // 2, lax.rem(t, 2)

            @pl.when(jnp.logical_not(is_own(i, c)))
            def _():
                cot_copy(h, i, c).start()

        inbuf[h, last, core] = outbuf[h, last, core]

    row = lax.broadcasted_iota(jnp.int32, (BV, channels), 0)
    by = lax.rem(row // 4, 4)
    bz = lax.rem(row, 4)
    keep = (by > 0, by < 3, bz > 0, bz < 3)
    own_shift = (4, 60, 1, 63)
    side_shift = (52, 12, 61, 3)

    @pl.loop(0, slots)
    def _(b):
        blk = feat[b]
        wide = blk.astype(F32)
        taps[b, :, 0:channels] = blk
        taps[b, 16:64, channels : 2 * channels] = blk[0:48]
        taps[b, 0:48, 2 * channels : 3 * channels] = blk[16:64]
        for k in range(4):
            n = jnp.minimum(nbr_s[2 + k, 0, b], slots)
            side = feat[n].astype(F32)
            tap = jnp.where(
                keep[k], pltpu.roll(wide, own_shift[k], 0), pltpu.roll(side, side_shift[k], 0)
            )
            taps[b, :, (3 + k) * channels : (4 + k) * channels] = tap.astype(BF16)

    halo_right.wait_recv()
    halo_left.wait_recv()

    @pl.loop(0, slots)
    def _(b):
        nm = jnp.minimum(nbr_s[0, 0, b], 2 * slots)
        np_ = nbr_s[1, 0, b]
        np_ = jnp.where(np_ < slots, np_, jnp.minimum(jnp.maximum(np_ - slots, slots), 2 * slots))
        taps[b, 0:16, channels : 2 * channels] = ext_m[nm]
        taps[b, 48:64, 2 * channels : 3 * channels] = ext_p[np_]

    @pl.loop(0, nz)
    def _(i):
        zs = lax.rem(z + offset(i), nz)
        for e in range(2):
            s = zs * 2 + e
            for k in range(7):
                cols = slice(k * channels, (k + 1) * channels)
                pair = jnp.concatenate(
                    [taps[send_s[0, 0, 0, s], :, cols], taps[send_s[0, 0, 1, s], :, cols]], 0
                )
                taps_t[i, cols, e * LANES : (e + 1) * LANES] = pair.T

    load_w.wait()
    live = counts_s[0, 0] * BV

    @pl.loop(0, slots // 4)
    def _(t):
        rows = taps[pl.ds(t * 4, 4)].reshape(4 * BV, taps_w)
        conv = jnp.dot(rows, w[...], preferred_element_type=F32)
        index = lax.broadcasted_iota(jnp.int32, (4 * BV, channels), 0) + t * (4 * BV)
        conv = jnp.where(index < live, conv, 0.0)
        vout[pl.ds(t * 4, 4)] = conv.astype(BF16).reshape(4, BV, channels)

    store_out = pltpu.make_async_copy(vout, out_hbm, local_sem.at[3])
    store_out.start()

    def grad_places(h, first, end):
        for i in range(first, end):
            for e in range(2):
                if i == last:
                    @pl.when(e != core)
                    def _():
                        cot_arrival(h, i, e).wait_recv()
                else:
                    cot_arrival(h, i, e).wait_recv()
        for m in range(7):
            rows = slice(m * channels, (m + 1) * channels)
            term = jnp.zeros((channels, LANES), F32) if first == 0 else acc[h, rows, :]
            for i in range(first, end):
                term += jnp.dot(
                    taps_t[i, rows, :], inbuf[h, i].reshape(2 * LANES, LANES), preferred_element_type=F32
                )
            acc[h, rows, :] = term

    def half_rows(c):
        return pl.ds(pl.multiple_of(c * half, 16), half)

    def core_copy(h):
        return remote(core_out.at[h], core_in.at[h], core_ss.at[h], core_rs.at[h], sibling)

    def x_copy(h, d):
        return remote(x_out.at[h, d], x_in.at[h, d], x_ss.at[h, d], x_rs.at[h, d], x_peer(d))

    def y_copy(h, d):
        return remote(y_out.at[h, d], y_in.at[h, d], y_ss.at[h, d], y_rs.at[h, d], y_peer(d))

    def z_copy(h, d):
        return remote(zbuf.at[h, z], zbuf.at[h, z], z_ss.at[h, d], z_rs.at[h, d], z_peer(d))

    def z_arrival(h, d):
        zs = lax.rem(z - d + nz, nz)
        return remote(zbuf.at[h, zs], zbuf.at[h, zs], z_ss.at[h, d], z_rs.at[h, d], z_peer(d))

    def y_rows(v):
        return pl.ds(pl.multiple_of(v * yr, 16), yr)

    def yg_copy(h, d):
        mine = ybuf.at[h, y_rows(y)]
        return remote(mine, mine, yg_ss.at[h, d], yg_rs.at[h, d], y_peer(d))

    def yg_arrival(h, d):
        theirs = ybuf.at[h, y_rows(lax.rem(y - d + ny, ny))]
        return remote(theirs, theirs, yg_ss.at[h, d], yg_rs.at[h, d], y_peer(d))

    def x_rows(v):
        return pl.ds(pl.multiple_of(core * half + v * xr, 16), xr)

    def xg_copy(h, d):
        mine = cbuf.at[h, x_rows(x)]
        return remote(mine, mine, xg_ss.at[h, d], xg_rs.at[h, d], x_peer(d))

    def xg_arrival(h, d):
        theirs = cbuf.at[h, x_rows(lax.rem(x - d + nx, nx))]
        return remote(theirs, theirs, xg_ss.at[h, d], xg_rs.at[h, d], x_peer(d))

    def cg_copy(h):
        mine = cbuf.at[h, half_rows(core)]
        return remote(mine, mine, cg_ss.at[h], cg_rs.at[h], sibling)

    def cg_arrival(h):
        theirs = cbuf.at[h, half_rows(1 - core)]
        return remote(theirs, theirs, cg_ss.at[h], cg_rs.at[h], sibling)

    def store_wg(h):
        return pltpu.make_async_copy(
            cbuf.at[h], wg_hbm.at[:, pl.ds(h * LANES, LANES)], local_sem.at[4 + h]
        )

    def sum_core(h):
        core_out[h] = acc[h, half_rows(1 - core), :].astype(BF16)
        core_copy(h).start()

    def sum_x(h):
        core_copy(h).wait_recv()
        acc[h, half_rows(core), :] += core_in[h].astype(F32)
        for d in range(1, nx):
            x_out[h, d] = acc[h, x_rows(lax.rem(x + d, nx)), :].astype(BF16)
            x_copy(h, d).start()

    def sum_y(h):
        total = acc[h, x_rows(x), :]
        for d in range(1, nx):
            x_copy(h, d).wait_recv()
            total += x_in[h, d].astype(F32)
        gx[h, 0:xr, :] = total
        if xr < ny * yr:
            gx[h, xr : ny * yr, :] = jnp.zeros((ny * yr - xr, LANES), F32)
        for d in range(1, ny):
            y_out[h, d] = gx[h, y_rows(lax.rem(y + d, ny)), :].astype(BF16)
            y_copy(h, d).start()

    def sum_z(h):
        total = gx[h, y_rows(y), :]
        for d in range(1, ny):
            y_copy(h, d).wait_recv()
            total += y_in[h, d].astype(F32)
        zbuf[h, z] = total.astype(BF16)
        for d in range(1, nz):
            z_copy(h, d).start()

    def spread_y(h):
        for d in range(1, nz):
            z_arrival(h, d).wait_recv()
        total = zbuf[h, 0].astype(F32)
        for v in range(1, nz):
            total += zbuf[h, v].astype(F32)
        ybuf[h, y_rows(y), :] = (total * scale).astype(BF16)
        for d in range(1, ny):
            yg_copy(h, d).start()

    def spread_x(h):
        for d in range(1, ny):
            yg_arrival(h, d).wait_recv()
        cbuf[h, x_rows(x), :] = ybuf[h, 0:xr, :]
        for d in range(1, nx):
            xg_copy(h, d).start()

    def spread_core(h):
        for d in range(1, nx):
            xg_arrival(h, d).wait_recv()
        cg_copy(h).start()

    def finish(h):
        cg_arrival(h).wait_recv()
        store_wg(h).start()

    steps = (sum_core, sum_x, sum_y, sum_z, spread_y, spread_x, spread_core, finish)
    lead = 3
    grad_places(0, 0, nz)
    for step in steps[:lead]:
        step(0)
    grad_places(1, 0, nz // 2)
    grad_places(1, nz // 2, nz)
    for i in range(len(steps)):
        steps[i](1)
        if i + lead < len(steps):
            steps[i + lead](0)

    halo_right.wait_send()
    halo_left.wait_send()
    for h in range(PARTS):
        @pl.loop(0, ns)
        def _(t):
            i, c = t // 2, lax.rem(t, 2)

            @pl.when(jnp.logical_not(is_own(i, c)))
            def _():
                cot_copy(h, i, c).wait_send()

        core_copy(h).wait_send()
        cg_copy(h).wait_send()
        for d in range(1, nx):
            x_copy(h, d).wait_send()
            xg_copy(h, d).wait_send()
        for d in range(1, ny):
            y_copy(h, d).wait_send()
            yg_copy(h, d).wait_send()
        for d in range(1, nz):
            z_copy(h, d).wait_send()
        store_wg(h).wait()
    store_out.wait()


def shards(dp_size, space_size, features, cotangent, weights, counts, neighbours, send_list, recv_list):
    slots, channels = features.shape[1], features.shape[-1]
    bal = cotangent.shape[1]
    ny = 1 << (dp_size.bit_length() // 2)
    nx = dp_size // ny
    nz = space_size // 2
    taps_w = 7 * channels
    half = taps_w // 2
    xr = half // nx
    yr = -(-xr // (16 * ny)) * 16
    scale = 1.0 / math.sqrt(dp_size * space_size * bal * BV)
    dma = pltpu.SemaphoreType.DMA
    vmem = pltpu.VMEM
    smem = pltpu.SMEM
    any_spec = pl.BlockSpec(memory_space=pl.ANY)
    macs = 2 * slots * BV * taps_w * channels
    voxel_out, weight_grad = pl.pallas_call(
        functools.partial(kernel, (nx, ny, nz, slots, bal, channels, scale)),
        out_shape=(
            jax.ShapeDtypeStruct((slots, BV, channels), BF16),
            jax.ShapeDtypeStruct((taps_w, channels), BF16),
        ),
        in_specs=[any_spec] * 3 + [pl.BlockSpec(memory_space=smem)] + [any_spec] * 3,
        out_specs=(any_spec, any_spec),
        scratch_shapes=[
            smem((6, 1, slots), jnp.int32),
            smem((1, 1, 2, space_size), jnp.int32),
            smem((1, bal), jnp.int32),
            vmem((bal, BV, channels), BF16),
            vmem((slots + 1, BV, channels), BF16),
            vmem((taps_w, channels), BF16),
            vmem((2 * slots + 1, 16, channels), BF16),
            vmem((2 * slots + 1, 16, channels), BF16),
            vmem((slots + 1, BV, taps_w), BF16),
            vmem((nz, taps_w, 2 * LANES), BF16),
            vmem((slots, BV, channels), BF16),
            vmem((PARTS, nz, 2, 2 * BV, LANES), BF16),
            vmem((PARTS, nz, 2, 2 * BV, LANES), BF16),
            vmem((PARTS, taps_w, LANES), F32),
            vmem((PARTS, half, LANES), BF16),
            vmem((PARTS, half, LANES), BF16),
            vmem((PARTS, nx, xr, LANES), BF16),
            vmem((PARTS, nx, xr, LANES), BF16),
            vmem((PARTS, ny * yr, LANES), F32),
            vmem((PARTS, ny, yr, LANES), BF16),
            vmem((PARTS, ny, yr, LANES), BF16),
            vmem((PARTS, nz, yr, LANES), BF16),
            vmem((PARTS, ny * yr, LANES), BF16),
            vmem((PARTS, taps_w, LANES), BF16),
            dma((7 + PARTS,)),
            dma((2,)),
            dma((2,)),
            dma((PARTS, nz, 2)),
            dma((PARTS, nz, 2)),
            dma((PARTS,)),
            dma((PARTS,)),
            dma((PARTS, nx)),
            dma((PARTS, nx)),
            dma((PARTS, ny)),
            dma((PARTS, ny)),
            dma((PARTS, nz)),
            dma((PARTS, nz)),
            dma((PARTS, ny)),
            dma((PARTS, ny)),
            dma((PARTS, nx)),
            dma((PARTS, nx)),
            dma((PARTS,)),
            dma((PARTS,)),
        ],
        compiler_params=pltpu.CompilerParams(
            collective_id=0, has_side_effects=True, vmem_limit_bytes=60 * 1024 * 1024
        ),
        cost_estimate=pl.CostEstimate(flops=4 * macs, bytes_accessed=6 << 20, transcendentals=0),
    )(
        cotangent[0], features[0], weights.reshape(taps_w, channels),
        counts, neighbours.transpose(2, 0, 1), send_list.transpose(0, 1, 3, 2), recv_list,
    )
    return voxel_out[None], weight_grad.reshape(7, channels, channels)


def solution(mesh):
    placed = (
        P("dp", "space", None, None),
        P("dp", "space", None, None),
        P(),
        P("dp", "space"),
        P("dp", "space", None),
        P("dp", "space", None, None),
        P("dp", "space"),
    )
    return jax.shard_map(
        functools.partial(shards, mesh.shape["dp"], mesh.shape["space"]),
        mesh=mesh,
        in_specs=placed,
        out_specs=(P("dp", "space", None, None), P()),
        check_vma=False,
    )
```

```python
import functools
import math

import jax
import jax.numpy as jnp
from jax import lax
from jax.experimental import pallas as pl
from jax.experimental.pallas import tpu as pltpu
from jax.sharding import PartitionSpec as P

MESH = pl.DeviceIdType.MESH
BV = 64
LANES = 128
PARTS = 2
F32 = jnp.float32
BF16 = jnp.bfloat16


def kernel(
    dims,
    cot_hbm, feat_hbm, w_hbm, counts_s, nbr_hbm, send_hbm, recv_hbm,
    out_hbm, wg_hbm,
    nbr_s, send_s, recv_s,
    cot, feat, w, ext_m, ext_p, taps, taps_t, vout,
    outbuf, inbuf, acc,
    core_out, core_in, x_out, x_in, gx, y_out, y_in, zbuf, cbuf,
    local_sem, halo_ss, halo_rs, cot_ss, cot_rs,
    core_ss, core_rs, x_ss, x_rs, y_ss, y_rs, z_ss, z_rs,
    yg_ss, yg_rs, xg_ss, xg_rs, cg_ss, cg_rs,
):
    nx, ny, nz, slots, bal, channels, scale = dims
    ns = 2 * nz
    taps_w = 7 * channels
    half = taps_w // 2
    xr = half // nx
    yr = gx.shape[1] // ny
    dp = lax.axis_index("dp")
    me = lax.axis_index("space")
    x, y = dp // ny, dp % ny
    z, core = me // 2, me % 2

    def remote(src, dst, ss, rs, dev):
        return pltpu.make_async_remote_copy(
            src_ref=src, dst_ref=dst, send_sem=ss, recv_sem=rs, device_id=dev, device_id_type=MESH
        )

    def space_peer(s):
        return (dp, s)

    def x_peer(d):
        return (lax.rem(x + d, nx) * ny + y, me)

    def y_peer(d):
        return (x * ny + lax.rem(y + d, ny), me)

    def z_peer(d):
        return (dp, lax.rem(z + d, nz) * 2 + core)

    sibling = (dp, z * 2 + (1 - core))

    barrier = pltpu.get_barrier_semaphore()

    @pl.loop(1, ns)
    def _(i):
        pl.semaphore_signal(barrier, inc=1, device_id=space_peer(lax.rem(me + i, ns)), device_id_type=MESH)

    @pl.loop(1, nx)
    def _(i):
        pl.semaphore_signal(barrier, inc=1, device_id=x_peer(i), device_id_type=MESH)

    @pl.loop(1, ny)
    def _(i):
        pl.semaphore_signal(barrier, inc=1, device_id=y_peer(i), device_id_type=MESH)

    load_cot = pltpu.make_async_copy(cot_hbm, cot, local_sem.at[0])
    load_feat = pltpu.make_async_copy(feat_hbm, feat.at[pl.ds(0, slots)], local_sem.at[1])
    load_w = pltpu.make_async_copy(w_hbm, w, local_sem.at[2])
    small = [
        pltpu.make_async_copy(src, dst, local_sem.at[4 + PARTS + i])
        for i, (src, dst) in enumerate(
            ((recv_hbm, recv_s), (nbr_hbm, nbr_s), (send_hbm, send_s))
        )
    ]
    for copy in small:
        copy.start()
    load_cot.start()
    load_feat.start()
    load_w.start()

    def offset(i):
        k = (i + 1) // 2
        return lax.rem(nz // 2 + k * (1 - 2 * lax.rem(i, 2)) + nz, nz)

    last = nz - 1

    feat[slots] = jnp.zeros((BV, channels), BF16)
    taps[slots] = jnp.zeros((BV, taps_w), BF16)
    ext_m[2 * slots] = jnp.zeros((16, channels), BF16)
    ext_p[2 * slots] = jnp.zeros((16, channels), BF16)

    for copy in small:
        copy.wait()
    load_cot.wait()

    load_feat.wait()

    @pl.loop(0, slots)
    def _(b):
        ext_m[b] = feat[b, 48:64, :]
        ext_p[b] = feat[b, 0:16, :]

    pl.semaphore_wait(barrier, ns - 1 + nx - 1 + ny - 1)

    halo_right = remote(
        ext_m.at[pl.ds(0, slots)], ext_m.at[pl.ds(slots, slots)], halo_ss.at[0], halo_rs.at[0],
        space_peer(lax.rem(me + 1, ns)),
    )
    halo_left = remote(
        ext_p.at[pl.ds(0, slots)], ext_p.at[pl.ds(slots, slots)], halo_ss.at[1], halo_rs.at[1],
        space_peer(lax.rem(me + ns - 1, ns)),
    )
    halo_right.start()
    halo_left.start()

    def cot_copy(h, i, c):
        dest = lax.rem(z - offset(i) + nz, nz) * 2 + c
        return remote(outbuf.at[h, i, c], inbuf.at[h, i, core], cot_ss.at[h, i, c], cot_rs.at[h, i, core], space_peer(dest))

    def cot_arrival(h, i, e):
        return remote(outbuf.at[h, i, e], inbuf.at[h, i, e], cot_ss.at[h, i, e], cot_rs.at[h, i, e], sibling)

    def is_own(i, c):
        return (i == last) & (c == core)

    @pl.loop(0, ns)
    def _(t):
        i, c = t // 2, lax.rem(t, 2)
        dest = lax.rem(z - offset(i) + nz, nz) * 2 + c
        for place in range(2):
            wanted = dest * 2 + place
            pos = jnp.int32(0)
            for r in range(bal):
                pos = jnp.where(recv_s[0, r] == wanted, r, pos)
            block = cot[pos]
            for h in range(PARTS):
                outbuf[h, i, c, pl.ds(place * BV, BV), :] = block[:, h * LANES : (h + 1) * LANES]

        @pl.when(jnp.logical_not(is_own(i, c)))
        def _():
            cot_copy(0, i, c).start()

    inbuf[0, last, core] = outbuf[0, last, core]
    row = lax.broadcasted_iota(jnp.int32, (BV, channels), 0)
    by = lax.rem(row // 4, 4)
    bz = lax.rem(row, 4)
    keep = (by > 0, by < 3, bz > 0, bz < 3)
    own_shift = (4, 60, 1, 63)
    side_shift = (52, 12, 61, 3)

    @pl.loop(0, slots)
    def _(b):
        blk = feat[b]
        wide = blk.astype(F32)
        taps[b, :, 0:channels] = blk
        taps[b, 16:64, channels : 2 * channels] = blk[0:48]
        taps[b, 0:48, 2 * channels : 3 * channels] = blk[16:64]
        for k in range(4):
            n = jnp.minimum(nbr_s[2 + k, 0, b], slots)
            side = feat[n].astype(F32)
            tap = jnp.where(
                keep[k], pltpu.roll(wide, own_shift[k], 0), pltpu.roll(side, side_shift[k], 0)
            )
            taps[b, :, (3 + k) * channels : (4 + k) * channels] = tap.astype(BF16)

    halo_right.wait_recv()
    halo_left.wait_recv()

    @pl.loop(0, slots)
    def _(b):
        nm = jnp.minimum(nbr_s[0, 0, b], 2 * slots)
        np_ = nbr_s[1, 0, b]
        np_ = jnp.where(np_ < slots, np_, jnp.minimum(jnp.maximum(np_ - slots, slots), 2 * slots))
        taps[b, 0:16, channels : 2 * channels] = ext_m[nm]
        taps[b, 48:64, 2 * channels : 3 * channels] = ext_p[np_]

    @pl.loop(0, nz)
    def _(i):
        zs = lax.rem(z + offset(i), nz)
        for e in range(2):
            s = zs * 2 + e
            for k in range(7):
                cols = slice(k * channels, (k + 1) * channels)
                pair = jnp.concatenate(
                    [taps[send_s[0, 0, 0, s], :, cols], taps[send_s[0, 0, 1, s], :, cols]], 0
                )
                taps_t[i, cols, e * LANES : (e + 1) * LANES] = pair.T

    load_w.wait()
    live = counts_s[0, 0] * BV

    @pl.loop(0, slots // 4)
    def _(t):
        rows = taps[pl.ds(t * 4, 4)].reshape(4 * BV, taps_w)
        conv = jnp.dot(rows, w[...], preferred_element_type=F32)
        index = lax.broadcasted_iota(jnp.int32, (4 * BV, channels), 0) + t * (4 * BV)
        conv = jnp.where(index < live, conv, 0.0)
        vout[pl.ds(t * 4, 4)] = conv.astype(BF16).reshape(4, BV, channels)

    store_out = pltpu.make_async_copy(vout, out_hbm, local_sem.at[3])
    store_out.start()

    @pl.loop(0, ns)
    def _(t):
        i, c = t // 2, lax.rem(t, 2)

        @pl.when(jnp.logical_not(is_own(i, c)))
        def _():
            cot_copy(0, i, c).wait_send()
            cot_copy(1, i, c).start()

    inbuf[1, last, core] = outbuf[1, last, core]

    def await_places(h, first, end):
        for i in range(first, end):
            for e in range(2):
                if i == last:
                    @pl.when(e != core)
                    def _():
                        cot_arrival(h, i, e).wait_recv()
                else:
                    cot_arrival(h, i, e).wait_recv()

    def grad_places(h, first, end):
        await_places(h, first, end)
        for m in range(7):
            rows = slice(m * channels, (m + 1) * channels)
            acc[h, rows, :] = product(h, first, end, rows)

    def product(h, first, end, rows):
        term = None
        for i in range(first, end):
            part = jnp.dot(
                taps_t[i, rows, :], inbuf[h, i].reshape(2 * LANES, LANES), preferred_element_type=F32
            )
            term = part if term is None else term + part
        return term

    def ring(n):
        return sorted(range(1, n), key=lambda d: min(d, n - d))

    def core_copy(h, d):
        return remote(core_out.at[h, d], core_in.at[h, d], core_ss.at[h, d], core_rs.at[h, d], sibling)

    def x_copy(h, d):
        return remote(x_out.at[h, d], x_in.at[h, d], x_ss.at[h, d], x_rs.at[h, d], x_peer(d))

    def y_copy(h, d):
        return remote(y_out.at[h, d], y_in.at[h, d], y_ss.at[h, d], y_rs.at[h, d], y_peer(d))

    def z_copy(h, d):
        return remote(zbuf.at[h, z], zbuf.at[h, z], z_ss.at[h, d], z_rs.at[h, d], z_peer(d))

    def z_arrival(h, d):
        zs = lax.rem(z - d + nz, nz)
        return remote(zbuf.at[h, zs], zbuf.at[h, zs], z_ss.at[h, d], z_rs.at[h, d], z_peer(d))

    def y_rows(v):
        return pl.ds(pl.multiple_of(v * yr, 16), yr)

    whole = xr // yr

    def piece(v, u, rows=yr):
        return pl.ds(pl.multiple_of(core * half + v * xr + u * yr, 16), rows)

    def yg_copy(h, d):
        mine = cbuf.at[h, piece(x, y)]
        return remote(mine, mine, yg_ss.at[h, d], yg_rs.at[h, d], y_peer(d))

    def yg_arrival(h, d):
        theirs = cbuf.at[h, piece(x, lax.rem(y - d + ny, ny))]
        return remote(theirs, theirs, yg_ss.at[h, d], yg_rs.at[h, d], y_peer(d))

    def xg_copy(h, u, d):
        mine = cbuf.at[h, piece(x, u)]
        return remote(mine, mine, xg_ss.at[h, u, d], xg_rs.at[h, u, d], x_peer(d))

    def xg_arrival(h, u, d):
        theirs = cbuf.at[h, piece(lax.rem(x - d + nx, nx), u)]
        return remote(theirs, theirs, xg_ss.at[h, u, d], xg_rs.at[h, u, d], x_peer(d))

    def cg_copy(h, d):
        mine = cbuf.at[h, piece(lax.rem(x - d + nx, nx), 0, xr)]
        return remote(mine, mine, cg_ss.at[h, d], cg_rs.at[h, d], sibling)

    def cg_arrival(h, d):
        start = (1 - core) * half + lax.rem(x - d + nx, nx) * xr
        theirs = cbuf.at[h, pl.ds(pl.multiple_of(start, 16), xr)]
        return remote(theirs, theirs, cg_ss.at[h, d], cg_rs.at[h, d], sibling)

    def store_wg(h):
        return pltpu.make_async_copy(
            cbuf.at[h], wg_hbm.at[:, pl.ds(h * LANES, LANES)], local_sem.at[4 + h]
        )

    def grad_x(h, first, begun):
        await_places(h, first, nz)
        order = ring(nx)[::-1] + [0]

        def rows_of(c, d):
            start = c * half + lax.rem(x + d, nx) * xr
            return pl.ds(pl.multiple_of(start, 16), xr)

        def total(c, d):
            term = product(h, first, nz, rows_of(c, d))
            return term + acc[h, rows_of(c, d), :] if begun else term

        for d in order:
            core_out[h, d] = total(1 - core, d).astype(BF16)
            core_copy(h, d).start()
        for d in order:
            term = total(core, d)
            core_copy(h, d).wait_recv()
            term += core_in[h, d].astype(F32)
            if d:
                x_out[h, d] = term.astype(BF16)
                x_copy(h, d).start()
            else:
                gx[h, 0:xr, :] = term

    def sum_y(h):
        total = gx[h, 0:xr, :]
        for d in ring(nx):
            x_copy(h, d).wait_recv()
            total += x_in[h, d].astype(F32)
        gx[h, 0:xr, :] = total
        if xr < ny * yr:
            gx[h, xr : ny * yr, :] = jnp.zeros((ny * yr - xr, LANES), F32)
        for d in ring(ny)[::-1]:
            y_out[h, d] = gx[h, y_rows(lax.rem(y + d, ny)), :].astype(BF16)
            y_copy(h, d).start()

    def sum_z(h):
        total = gx[h, y_rows(y), :]
        for d in ring(ny):
            y_copy(h, d).wait_recv()
            total += y_in[h, d].astype(F32)
        zbuf[h, z] = total.astype(BF16)
        for d in ring(nz)[::-1]:
            z_copy(h, d).start()

    def spread_y(h):
        for d in range(1, nz):
            z_arrival(h, d).wait_recv()
        total = zbuf[h, 0].astype(F32)
        for v in range(1, nz):
            total += zbuf[h, v].astype(F32)

        @pl.when(y < whole)
        def _():
            cbuf[h, piece(x, y), :] = (total * scale).astype(BF16)
            for d in ring(ny)[::-1]:
                yg_copy(h, d).start()
            for d in ring(nx)[::-1]:
                xg_copy(h, y, d).start()

    def spread_x(h):
        for d in ring(ny):
            u = lax.rem(y - d + ny, ny)

            @pl.when(u < whole)
            def _():
                yg_arrival(h, d).wait_recv()
                for v in ring(nx)[::-1]:
                    xg_copy(h, u, v).start()
        cg_copy(h, 0).start()

    def spread_core(h):
        for d in ring(nx):
            @pl.loop(0, whole)
            def _(u):
                xg_arrival(h, u, d).wait_recv()

            cg_copy(h, d).start()

    def finish(h):
        for d in [0] + ring(nx):
            cg_arrival(h, d).wait_recv()
        store_wg(h).start()

    grad_x(0, 0, False)
    sum_y(0)
    grad_places(1, 0, nz // 2)
    grad_x(1, nz // 2, True)
    sum_z(0)
    sum_y(1)
    spread_y(0)
    sum_z(1)
    spread_x(0)
    spread_y(1)
    spread_core(0)
    spread_x(1)
    finish(0)
    spread_core(1)
    finish(1)

    halo_right.wait_send()
    halo_left.wait_send()
    @pl.loop(0, ns)
    def _(t):
        i, c = t // 2, lax.rem(t, 2)

        @pl.when(jnp.logical_not(is_own(i, c)))
        def _():
            cot_copy(PARTS - 1, i, c).wait_send()

    for h in range(PARTS):
        for d in range(nx):
            core_copy(h, d).wait_send()
            cg_copy(h, d).wait_send()
        for d in range(1, nx):
            x_copy(h, d).wait_send()

            @pl.loop(0, whole)
            def _(u):
                xg_copy(h, u, d).wait_send()
        for d in range(1, ny):
            y_copy(h, d).wait_send()

            @pl.when(y < whole)
            def _():
                yg_copy(h, d).wait_send()
        for d in range(1, nz):
            z_copy(h, d).wait_send()
        store_wg(h).wait()
    store_out.wait()


def shards(dp_size, space_size, features, cotangent, weights, counts, neighbours, send_list, recv_list):
    slots, channels = features.shape[1], features.shape[-1]
    bal = cotangent.shape[1]
    ny = 1 << (dp_size.bit_length() // 2)
    nx = dp_size // ny
    nz = space_size // 2
    taps_w = 7 * channels
    half = taps_w // 2
    xr = half // nx
    yr = -(-xr // (16 * ny)) * 16
    scale = 1.0 / math.sqrt(dp_size * space_size * bal * BV)
    dma = pltpu.SemaphoreType.DMA
    vmem = pltpu.VMEM
    smem = pltpu.SMEM
    any_spec = pl.BlockSpec(memory_space=pl.ANY)
    macs = 2 * slots * BV * taps_w * channels
    voxel_out, weight_grad = pl.pallas_call(
        functools.partial(kernel, (nx, ny, nz, slots, bal, channels, scale)),
        out_shape=(
            jax.ShapeDtypeStruct((slots, BV, channels), BF16),
            jax.ShapeDtypeStruct((taps_w, channels), BF16),
        ),
        in_specs=[any_spec] * 3 + [pl.BlockSpec(memory_space=smem)] + [any_spec] * 3,
        out_specs=(any_spec, any_spec),
        scratch_shapes=[
            smem((6, 1, slots), jnp.int32),
            smem((1, 1, 2, space_size), jnp.int32),
            smem((1, bal), jnp.int32),
            vmem((bal, BV, channels), BF16),
            vmem((slots + 1, BV, channels), BF16),
            vmem((taps_w, channels), BF16),
            vmem((2 * slots + 1, 16, channels), BF16),
            vmem((2 * slots + 1, 16, channels), BF16),
            vmem((slots + 1, BV, taps_w), BF16),
            vmem((nz, taps_w, 2 * LANES), BF16),
            vmem((slots, BV, channels), BF16),
            vmem((PARTS, nz, 2, 2 * BV, LANES), BF16),
            vmem((PARTS, nz, 2, 2 * BV, LANES), BF16),
            vmem((PARTS, taps_w, LANES), F32),
            vmem((PARTS, nx, xr, LANES), BF16),
            vmem((PARTS, nx, xr, LANES), BF16),
            vmem((PARTS, nx, xr, LANES), BF16),
            vmem((PARTS, nx, xr, LANES), BF16),
            vmem((PARTS, ny * yr, LANES), F32),
            vmem((PARTS, ny, yr, LANES), BF16),
            vmem((PARTS, ny, yr, LANES), BF16),
            vmem((PARTS, nz, yr, LANES), BF16),
            vmem((PARTS, taps_w, LANES), BF16),
            dma((7 + PARTS,)),
            dma((2,)),
            dma((2,)),
            dma((PARTS, nz, 2)),
            dma((PARTS, nz, 2)),
            dma((PARTS, nx)),
            dma((PARTS, nx)),
            dma((PARTS, nx)),
            dma((PARTS, nx)),
            dma((PARTS, ny)),
            dma((PARTS, ny)),
            dma((PARTS, nz)),
            dma((PARTS, nz)),
            dma((PARTS, ny)),
            dma((PARTS, ny)),
            dma((PARTS, ny, nx)),
            dma((PARTS, ny, nx)),
            dma((PARTS, nx)),
            dma((PARTS, nx)),
        ],
        compiler_params=pltpu.CompilerParams(
            collective_id=0, has_side_effects=True, vmem_limit_bytes=60 * 1024 * 1024
        ),
        cost_estimate=pl.CostEstimate(flops=4 * macs, bytes_accessed=6 << 20, transcendentals=0),
    )(
        cotangent[0], features[0], weights.reshape(taps_w, channels),
        counts, neighbours.transpose(2, 0, 1), send_list.transpose(0, 1, 3, 2), recv_list,
    )
    return voxel_out[None], weight_grad.reshape(7, channels, channels)


def solution(mesh):
    placed = (
        P("dp", "space", None, None),
        P("dp", "space", None, None),
        P(),
        P("dp", "space"),
        P("dp", "space", None),
        P("dp", "space", None, None),
        P("dp", "space"),
    )
    return jax.shard_map(
        functools.partial(shards, mesh.shape["dp"], mesh.shape["space"]),
        mesh=mesh,
        in_specs=placed,
        out_specs=(P("dp", "space", None, None), P()),
        check_vma=False,
    )
```

```python
import functools
import math

import jax
import jax.numpy as jnp
from jax import lax
from jax.experimental import pallas as pl
from jax.experimental.pallas import tpu as pltpu
from jax.sharding import PartitionSpec as P

MESH = pl.DeviceIdType.MESH
BV = 64
LANES = 128
PARTS = 2
F32 = jnp.float32
BF16 = jnp.bfloat16


def kernel(
    dims,
    cot_hbm, feat_hbm, w_hbm, counts_s, nbr_hbm, send_hbm, recv_hbm,
    out_hbm, wg_hbm,
    nbr_s, send_s, recv_s,
    cot, feat, w, ext_m, ext_p, taps, taps_t, vout,
    outbuf, inbuf, acc,
    core_out, core_in, x_out, x_in, gx, y_out, y_in, zbuf, cbuf,
    local_sem, halo_ss, halo_rs, cot_ss, cot_rs,
    core_ss, core_rs, x_ss, x_rs, y_ss, y_rs, z_ss, z_rs,
    yg_ss, yg_rs, xg_ss, xg_rs, cg_ss, cg_rs,
):
    nx, ny, nz, slots, bal, channels, scale = dims
    ns = 2 * nz
    taps_w = 7 * channels
    half = taps_w // 2
    xr = half // nx
    yr = gx.shape[1] // ny
    dp = lax.axis_index("dp")
    me = lax.axis_index("space")
    x, y = dp // ny, dp % ny
    z, core = me // 2, me % 2

    def remote(src, dst, ss, rs, dev):
        return pltpu.make_async_remote_copy(
            src_ref=src, dst_ref=dst, send_sem=ss, recv_sem=rs, device_id=dev, device_id_type=MESH
        )

    def space_peer(s):
        return (dp, s)

    def x_peer(d):
        return (lax.rem(x + d, nx) * ny + y, me)

    def y_peer(d):
        return (x * ny + lax.rem(y + d, ny), me)

    def z_peer(d):
        return (dp, lax.rem(z + d, nz) * 2 + core)

    sibling = (dp, z * 2 + (1 - core))

    barrier = pltpu.get_barrier_semaphore()

    @pl.loop(1, ns)
    def _(i):
        pl.semaphore_signal(barrier, inc=1, device_id=space_peer(lax.rem(me + i, ns)), device_id_type=MESH)

    @pl.loop(1, nx)
    def _(i):
        pl.semaphore_signal(barrier, inc=1, device_id=x_peer(i), device_id_type=MESH)

    @pl.loop(1, ny)
    def _(i):
        pl.semaphore_signal(barrier, inc=1, device_id=y_peer(i), device_id_type=MESH)

    load_cot = pltpu.make_async_copy(cot_hbm, cot, local_sem.at[0])
    load_feat = pltpu.make_async_copy(feat_hbm, feat.at[pl.ds(0, slots)], local_sem.at[1])
    load_w = pltpu.make_async_copy(w_hbm, w, local_sem.at[2])
    small = [
        pltpu.make_async_copy(src, dst, local_sem.at[4 + PARTS + i])
        for i, (src, dst) in enumerate(
            ((recv_hbm, recv_s), (nbr_hbm, nbr_s), (send_hbm, send_s))
        )
    ]
    for copy in small:
        copy.start()
    load_cot.start()
    load_feat.start()
    load_w.start()

    def offset(i):
        k = (i + 1) // 2
        return lax.rem(nz // 2 + k * (1 - 2 * lax.rem(i, 2)) + nz, nz)

    last = nz - 1

    feat[slots] = jnp.zeros((BV, channels), BF16)
    taps[slots] = jnp.zeros((BV, taps_w), BF16)
    ext_m[2 * slots] = jnp.zeros((16, channels), BF16)
    ext_p[2 * slots] = jnp.zeros((16, channels), BF16)

    for copy in small:
        copy.wait()
    load_cot.wait()

    load_feat.wait()

    @pl.loop(0, slots)
    def _(b):
        ext_m[b] = feat[b, 48:64, :]
        ext_p[b] = feat[b, 0:16, :]

    pl.semaphore_wait(barrier, ns - 1 + nx - 1 + ny - 1)

    halo_right = remote(
        ext_m.at[pl.ds(0, slots)], ext_m.at[pl.ds(slots, slots)], halo_ss.at[0], halo_rs.at[0],
        space_peer(lax.rem(me + 1, ns)),
    )
    halo_left = remote(
        ext_p.at[pl.ds(0, slots)], ext_p.at[pl.ds(slots, slots)], halo_ss.at[1], halo_rs.at[1],
        space_peer(lax.rem(me + ns - 1, ns)),
    )
    halo_right.start()
    halo_left.start()

    def cot_copy(h, i, c):
        dest = lax.rem(z - offset(i) + nz, nz) * 2 + c
        return remote(outbuf.at[h, i, c], inbuf.at[h, i, core], cot_ss.at[h, i, c], cot_rs.at[h, i, core], space_peer(dest))

    def cot_arrival(h, i, e):
        return remote(outbuf.at[h, i, e], inbuf.at[h, i, e], cot_ss.at[h, i, e], cot_rs.at[h, i, e], sibling)

    def is_own(i, c):
        return (i == last) & (c == core)

    @pl.loop(0, ns)
    def _(t):
        i, c = t // 2, lax.rem(t, 2)
        dest = lax.rem(z - offset(i) + nz, nz) * 2 + c
        for place in range(2):
            wanted = dest * 2 + place
            pos = jnp.int32(0)
            for r in range(bal):
                pos = jnp.where(recv_s[0, r] == wanted, r, pos)
            block = cot[pos]
            for h in range(PARTS):
                outbuf[h, i, c, pl.ds(place * BV, BV), :] = block[:, h * LANES : (h + 1) * LANES]

        @pl.when(jnp.logical_not(is_own(i, c)))
        def _():
            cot_copy(0, i, c).start()

    inbuf[0, last, core] = outbuf[0, last, core]
    row = lax.broadcasted_iota(jnp.int32, (BV, channels), 0)
    by = lax.rem(row // 4, 4)
    bz = lax.rem(row, 4)
    keep = (by > 0, by < 3, bz > 0, bz < 3)
    own_shift = (4, 60, 1, 63)
    side_shift = (52, 12, 61, 3)

    @pl.loop(0, slots)
    def _(b):
        blk = feat[b]
        wide = blk.astype(F32)
        taps[b, :, 0:channels] = blk
        taps[b, 16:64, channels : 2 * channels] = blk[0:48]
        taps[b, 0:48, 2 * channels : 3 * channels] = blk[16:64]
        for k in range(4):
            n = jnp.minimum(nbr_s[2 + k, 0, b], slots)
            side = feat[n].astype(F32)
            tap = jnp.where(
                keep[k], pltpu.roll(wide, own_shift[k], 0), pltpu.roll(side, side_shift[k], 0)
            )
            taps[b, :, (3 + k) * channels : (4 + k) * channels] = tap.astype(BF16)

    halo_right.wait_recv()
    halo_left.wait_recv()

    @pl.loop(0, slots)
    def _(b):
        nm = jnp.minimum(nbr_s[0, 0, b], 2 * slots)
        np_ = nbr_s[1, 0, b]
        np_ = jnp.where(np_ < slots, np_, jnp.minimum(jnp.maximum(np_ - slots, slots), 2 * slots))
        taps[b, 0:16, channels : 2 * channels] = ext_m[nm]
        taps[b, 48:64, 2 * channels : 3 * channels] = ext_p[np_]

    @pl.loop(0, nz)
    def _(i):
        zs = lax.rem(z + offset(i), nz)
        for e in range(2):
            s = zs * 2 + e
            for k in range(7):
                cols = slice(k * channels, (k + 1) * channels)
                pair = jnp.concatenate(
                    [taps[send_s[0, 0, 0, s], :, cols], taps[send_s[0, 0, 1, s], :, cols]], 0
                )
                taps_t[i, cols, e * LANES : (e + 1) * LANES] = pair.T

    load_w.wait()
    live = counts_s[0, 0] * BV

    @pl.loop(0, slots // 4)
    def _(t):
        rows = taps[pl.ds(t * 4, 4)].reshape(4 * BV, taps_w)
        conv = jnp.dot(rows, w[...], preferred_element_type=F32)
        index = lax.broadcasted_iota(jnp.int32, (4 * BV, channels), 0) + t * (4 * BV)
        conv = jnp.where(index < live, conv, 0.0)
        vout[pl.ds(t * 4, 4)] = conv.astype(BF16).reshape(4, BV, channels)

    store_out = pltpu.make_async_copy(vout, out_hbm, local_sem.at[3])
    store_out.start()

    @pl.loop(0, ns)
    def _(t):
        i, c = t // 2, lax.rem(t, 2)

        @pl.when(jnp.logical_not(is_own(i, c)))
        def _():
            cot_copy(0, i, c).wait_send()
            cot_copy(1, i, c).start()

    inbuf[1, last, core] = outbuf[1, last, core]

    def await_places(h, first, end):
        for i in range(first, end):
            for e in range(2):
                if i == last:
                    @pl.when(e != core)
                    def _():
                        cot_arrival(h, i, e).wait_recv()
                else:
                    cot_arrival(h, i, e).wait_recv()

    def grad_places(h, first, end):
        await_places(h, first, end)
        for m in range(7):
            rows = slice(m * channels, (m + 1) * channels)
            acc[h, rows, :] = product(h, first, end, rows)

    def product(h, first, end, rows):
        term = None
        for i in range(first, end):
            part = jnp.dot(
                taps_t[i, rows, :], inbuf[h, i].reshape(2 * LANES, LANES), preferred_element_type=F32
            )
            term = part if term is None else term + part
        return term

    def ring(n):
        return sorted(range(1, n), key=lambda d: min(d, n - d))

    def core_copy(h, d):
        return remote(core_out.at[h, d], core_in.at[h, d], core_ss.at[h, d], core_rs.at[h, d], sibling)

    def x_copy(h, d):
        return remote(x_out.at[h, d], x_in.at[h, d], x_ss.at[h, d], x_rs.at[h, d], x_peer(d))

    def y_copy(h, d):
        return remote(y_out.at[h, d], y_in.at[h, d], y_ss.at[h, d], y_rs.at[h, d], y_peer(d))

    def z_copy(h, d):
        return remote(zbuf.at[h, z], zbuf.at[h, z], z_ss.at[h, d], z_rs.at[h, d], z_peer(d))

    def z_arrival(h, d):
        zs = lax.rem(z - d + nz, nz)
        return remote(zbuf.at[h, zs], zbuf.at[h, zs], z_ss.at[h, d], z_rs.at[h, d], z_peer(d))

    def y_rows(v):
        return pl.ds(pl.multiple_of(v * yr, 16), yr)

    whole = xr // yr

    def piece(v, u, rows=yr):
        return pl.ds(pl.multiple_of(core * half + v * xr + u * yr, 16), rows)

    def yg_copy(h, d):
        mine = cbuf.at[h, piece(x, y)]
        return remote(mine, mine, yg_ss.at[h, d], yg_rs.at[h, d], y_peer(d))

    def yg_arrival(h, d):
        theirs = cbuf.at[h, piece(x, lax.rem(y - d + ny, ny))]
        return remote(theirs, theirs, yg_ss.at[h, d], yg_rs.at[h, d], y_peer(d))

    def xg_copy(h, u, d):
        mine = cbuf.at[h, piece(x, u)]
        return remote(mine, mine, xg_ss.at[h, u, d], xg_rs.at[h, u, d], x_peer(d))

    def xg_arrival(h, u, d):
        theirs = cbuf.at[h, piece(lax.rem(x - d + nx, nx), u)]
        return remote(theirs, theirs, xg_ss.at[h, u, d], xg_rs.at[h, u, d], x_peer(d))

    def cg_copy(h, d):
        mine = cbuf.at[h, piece(lax.rem(x - d + nx, nx), 0, xr)]
        return remote(mine, mine, cg_ss.at[h, d], cg_rs.at[h, d], sibling)

    def cg_arrival(h, d):
        start = (1 - core) * half + lax.rem(x - d + nx, nx) * xr
        theirs = cbuf.at[h, pl.ds(pl.multiple_of(start, 16), xr)]
        return remote(theirs, theirs, cg_ss.at[h, d], cg_rs.at[h, d], sibling)

    def store_wg(h):
        return pltpu.make_async_copy(
            cbuf.at[h], wg_hbm.at[:, pl.ds(h * LANES, LANES)], local_sem.at[4 + h]
        )

    def settle_sums(h):
        for d in range(nx):
            core_copy(h, d).wait_send()
        for d in range(1, nx):
            x_copy(h, d).wait_send()
        for d in range(1, ny):
            y_copy(h, d).wait_send()
        for d in range(1, nz):
            z_copy(h, d).wait_send()

    def settle_gathers(h):
        for d in range(1, nx):
            @pl.loop(0, whole)
            def _(u):
                xg_copy(h, u, d).wait_send()
        for d in range(1, ny):
            @pl.when(y < whole)
            def _():
                yg_copy(h, d).wait_send()

    def settle_places():
        halo_right.wait_send()
        halo_left.wait_send()

        @pl.loop(0, ns)
        def _(t):
            i, c = t // 2, lax.rem(t, 2)

            @pl.when(jnp.logical_not(is_own(i, c)))
            def _():
                cot_copy(PARTS - 1, i, c).wait_send()

    def grad_x(h, first, begun):
        await_places(h, first, nz)
        order = ring(nx)[::-1] + [0]

        def rows_of(c, d):
            start = c * half + lax.rem(x + d, nx) * xr
            return pl.ds(pl.multiple_of(start, 16), xr)

        def total(c, d):
            term = product(h, first, nz, rows_of(c, d))
            return term + acc[h, rows_of(c, d), :] if begun else term

        for d in order:
            core_out[h, d] = total(1 - core, d).astype(BF16)
            core_copy(h, d).start()
        for d in order:
            term = total(core, d)
            core_copy(h, d).wait_recv()
            term += core_in[h, d].astype(F32)
            if d:
                x_out[h, d] = term.astype(BF16)
                x_copy(h, d).start()
            else:
                gx[h, 0:xr, :] = term

    def sum_y(h):
        total = gx[h, 0:xr, :]
        for d in ring(nx):
            x_copy(h, d).wait_recv()
            total += x_in[h, d].astype(F32)
        gx[h, 0:xr, :] = total
        if xr < ny * yr:
            gx[h, xr : ny * yr, :] = jnp.zeros((ny * yr - xr, LANES), F32)
        for d in ring(ny)[::-1]:
            y_out[h, d] = gx[h, y_rows(lax.rem(y + d, ny)), :].astype(BF16)
            y_copy(h, d).start()

    def sum_z(h):
        total = gx[h, y_rows(y), :]
        for d in ring(ny):
            y_copy(h, d).wait_recv()
            total += y_in[h, d].astype(F32)
        zbuf[h, z] = total.astype(BF16)
        for d in ring(nz)[::-1]:
            z_copy(h, d).start()

    def spread_y(h):
        for d in range(1, nz):
            z_arrival(h, d).wait_recv()
        total = zbuf[h, 0].astype(F32)
        for v in range(1, nz):
            total += zbuf[h, v].astype(F32)

        @pl.when(y < whole)
        def _():
            cbuf[h, piece(x, y), :] = (total * scale).astype(BF16)
            for d in ring(ny)[::-1]:
                yg_copy(h, d).start()
            for d in ring(nx)[::-1]:
                xg_copy(h, y, d).start()

    def spread_x(h):
        for d in ring(ny):
            u = lax.rem(y - d + ny, ny)

            @pl.when(u < whole)
            def _():
                yg_arrival(h, d).wait_recv()
                for v in ring(nx)[::-1]:
                    xg_copy(h, u, v).start()
        cg_copy(h, 0).start()

    def spread_core(h):
        for d in ring(nx):
            @pl.loop(0, whole)
            def _(u):
                xg_arrival(h, u, d).wait_recv()

            cg_copy(h, d).start()

    def finish(h):
        for d in [0] + ring(nx):
            cg_arrival(h, d).wait_recv()
        store_wg(h).start()

    grad_x(0, 0, False)
    sum_y(0)
    grad_places(1, 0, nz // 2)
    grad_x(1, nz // 2, True)
    sum_z(0)
    sum_y(1)
    spread_y(0)
    sum_z(1)
    spread_x(0)
    settle_places()
    settle_sums(0)
    spread_y(1)
    spread_core(0)
    spread_x(1)
    finish(0)
    settle_sums(1)
    settle_gathers(0)
    for d in range(nx):
        cg_copy(0, d).wait_send()
    spread_core(1)
    settle_gathers(1)
    finish(1)

    for d in range(nx):
        cg_copy(1, d).wait_send()
    for h in range(PARTS):
        store_wg(h).wait()
    store_out.wait()


def hand_over(out_in, wg_in, out, wg, out_mid, wg_mid, in_sem, out_sem):
    pairs = []
    for src, mid, dst in ((out_in, out_mid, out), (wg_in, wg_mid, wg)):
        step = src.shape[0] // 4
        for i in range(4):
            part = pl.ds(i * step, step)
            n = len(pairs)
            pairs.append(
                (
                    pltpu.make_async_copy(src.at[part], mid.at[part], in_sem.at[n]),
                    pltpu.make_async_copy(mid.at[part], dst.at[part], out_sem.at[n]),
                )
            )
    for load, _ in pairs:
        load.start()
    for load, store in pairs:
        load.wait()
        store.start()
    for _, store in pairs:
        store.wait()


def shards(dp_size, space_size, features, cotangent, weights, counts, neighbours, send_list, recv_list):
    slots, channels = features.shape[1], features.shape[-1]
    bal = cotangent.shape[1]
    ny = 1 << (dp_size.bit_length() // 2)
    nx = dp_size // ny
    nz = space_size // 2
    taps_w = 7 * channels
    half = taps_w // 2
    xr = half // nx
    yr = -(-xr // (16 * ny)) * 16
    scale = 1.0 / math.sqrt(dp_size * space_size * bal * BV)
    dma = pltpu.SemaphoreType.DMA
    vmem = pltpu.VMEM
    smem = pltpu.SMEM
    any_spec = pl.BlockSpec(memory_space=pl.ANY)
    macs = 2 * slots * BV * taps_w * channels
    voxel_out, weight_grad = pl.pallas_call(
        functools.partial(kernel, (nx, ny, nz, slots, bal, channels, scale)),
        out_shape=(
            jax.ShapeDtypeStruct((slots, BV, channels), BF16),
            jax.ShapeDtypeStruct((taps_w, channels), BF16),
        ),
        in_specs=[any_spec] * 3 + [pl.BlockSpec(memory_space=smem)] + [any_spec] * 3,
        out_specs=(any_spec, any_spec),
        scratch_shapes=[
            smem((6, 1, slots), jnp.int32),
            smem((1, 1, 2, space_size), jnp.int32),
            smem((1, bal), jnp.int32),
            vmem((bal, BV, channels), BF16),
            vmem((slots + 1, BV, channels), BF16),
            vmem((taps_w, channels), BF16),
            vmem((2 * slots + 1, 16, channels), BF16),
            vmem((2 * slots + 1, 16, channels), BF16),
            vmem((slots + 1, BV, taps_w), BF16),
            vmem((nz, taps_w, 2 * LANES), BF16),
            vmem((slots, BV, channels), BF16),
            vmem((PARTS, nz, 2, 2 * BV, LANES), BF16),
            vmem((PARTS, nz, 2, 2 * BV, LANES), BF16),
            vmem((PARTS, taps_w, LANES), F32),
            vmem((PARTS, nx, xr, LANES), BF16),
            vmem((PARTS, nx, xr, LANES), BF16),
            vmem((PARTS, nx, xr, LANES), BF16),
            vmem((PARTS, nx, xr, LANES), BF16),
            vmem((PARTS, ny * yr, LANES), F32),
            vmem((PARTS, ny, yr, LANES), BF16),
            vmem((PARTS, ny, yr, LANES), BF16),
            vmem((PARTS, nz, yr, LANES), BF16),
            vmem((PARTS, taps_w, LANES), BF16),
            dma((7 + PARTS,)),
            dma((2,)),
            dma((2,)),
            dma((PARTS, nz, 2)),
            dma((PARTS, nz, 2)),
            dma((PARTS, nx)),
            dma((PARTS, nx)),
            dma((PARTS, nx)),
            dma((PARTS, nx)),
            dma((PARTS, ny)),
            dma((PARTS, ny)),
            dma((PARTS, nz)),
            dma((PARTS, nz)),
            dma((PARTS, ny)),
            dma((PARTS, ny)),
            dma((PARTS, ny, nx)),
            dma((PARTS, ny, nx)),
            dma((PARTS, nx)),
            dma((PARTS, nx)),
        ],
        compiler_params=pltpu.CompilerParams(
            collective_id=0, has_side_effects=True, vmem_limit_bytes=60 * 1024 * 1024
        ),
        cost_estimate=pl.CostEstimate(flops=4 * macs, bytes_accessed=6 << 20, transcendentals=0),
    )(
        cotangent[0], features[0], weights.reshape(taps_w, channels),
        counts, neighbours.transpose(2, 0, 1), send_list.transpose(0, 1, 3, 2), recv_list,
    )
    voxel_out, weight_grad = pl.pallas_call(
        hand_over,
        out_shape=(
            jax.ShapeDtypeStruct(voxel_out.shape, BF16),
            jax.ShapeDtypeStruct(weight_grad.shape, BF16),
        ),
        in_specs=[any_spec] * 2,
        out_specs=(any_spec, any_spec),
        scratch_shapes=[
            vmem(voxel_out.shape, BF16),
            vmem(weight_grad.shape, BF16),
            dma((8,)),
            dma((8,)),
        ],
        compiler_params=pltpu.CompilerParams(vmem_limit_bytes=60 * 1024 * 1024),
    )(voxel_out, weight_grad)
    return voxel_out[None], weight_grad.reshape(7, channels, channels)


def solution(mesh):
    placed = (
        P("dp", "space", None, None),
        P("dp", "space", None, None),
        P(),
        P("dp", "space"),
        P("dp", "space", None),
        P("dp", "space", None, None),
        P("dp", "space"),
    )
    return jax.shard_map(
        functools.partial(shards, mesh.shape["dp"], mesh.shape["space"]),
        mesh=mesh,
        in_specs=placed,
        out_specs=(P("dp", "space", None, None), P()),
        check_vma=False,
    )
```

```python
import functools
import math

import jax
import jax.numpy as jnp
from jax import lax
from jax.experimental import pallas as pl
from jax.experimental.pallas import tpu as pltpu
from jax.sharding import PartitionSpec as P

MESH = pl.DeviceIdType.MESH
BV = 64
LANES = 128
PARTS = 2
F32 = jnp.float32
BF16 = jnp.bfloat16


def kernel(
    dims,
    cot_hbm, feat_hbm, w_hbm, counts_s, nbr_hbm, send_hbm, recv_hbm,
    out_hbm, wg_hbm,
    nbr_s, send_s, recv_s,
    cot, feat, w, ext_m, ext_p, taps, taps_t, vout,
    outbuf, inbuf, acc,
    core_out, core_in, x_out, x_in, gx, y_out, y_in, zbuf, cbuf,
    local_sem, halo_ss, halo_rs, cot_ss, cot_rs,
    core_ss, core_rs, x_ss, x_rs, y_ss, y_rs, z_ss, z_rs,
    yg_ss, yg_rs, xg_ss, xg_rs, cg_ss, cg_rs,
):
    nx, ny, nz, slots, bal, channels, scale = dims
    ns = 2 * nz
    taps_w = 7 * channels
    half = taps_w // 2
    xr = half // nx
    yr = gx.shape[1] // ny
    dp = lax.axis_index("dp")
    me = lax.axis_index("space")
    x, y = dp // ny, dp % ny
    z, core = me // 2, me % 2

    def remote(src, dst, ss, rs, dev):
        return pltpu.make_async_remote_copy(
            src_ref=src, dst_ref=dst, send_sem=ss, recv_sem=rs, device_id=dev, device_id_type=MESH
        )

    def space_peer(s):
        return (dp, s)

    def x_peer(d):
        return (lax.rem(x + d, nx) * ny + y, me)

    def y_peer(d):
        return (x * ny + lax.rem(y + d, ny), me)

    def z_peer(d):
        return (dp, lax.rem(z + d, nz) * 2 + core)

    sibling = (dp, z * 2 + (1 - core))

    barrier = pltpu.get_barrier_semaphore()

    @pl.loop(1, ns)
    def _(i):
        pl.semaphore_signal(barrier, inc=1, device_id=space_peer(lax.rem(me + i, ns)), device_id_type=MESH)

    @pl.loop(1, nx)
    def _(i):
        pl.semaphore_signal(barrier, inc=1, device_id=x_peer(i), device_id_type=MESH)

    @pl.loop(1, ny)
    def _(i):
        pl.semaphore_signal(barrier, inc=1, device_id=y_peer(i), device_id_type=MESH)

    load_cot = pltpu.make_async_copy(cot_hbm, cot, local_sem.at[0])
    load_feat = pltpu.make_async_copy(feat_hbm, feat.at[pl.ds(0, slots)], local_sem.at[1])
    load_w = pltpu.make_async_copy(w_hbm, w, local_sem.at[2])
    small = [
        pltpu.make_async_copy(src, dst, local_sem.at[4 + PARTS + i])
        for i, (src, dst) in enumerate(
            ((recv_hbm, recv_s), (nbr_hbm, nbr_s), (send_hbm, send_s))
        )
    ]
    for copy in small:
        copy.start()
    load_cot.start()
    load_feat.start()
    load_w.start()

    def offset(i):
        k = i // 2 + 1
        return lax.rem(k * (1 - 2 * lax.rem(i, 2)) + nz, nz) * (1 - i // (nz - 1))

    last = nz - 1

    feat[slots] = jnp.zeros((BV, channels), BF16)
    taps[slots] = jnp.zeros((BV, taps_w), BF16)
    ext_m[2 * slots] = jnp.zeros((16, channels), BF16)
    ext_p[2 * slots] = jnp.zeros((16, channels), BF16)

    for copy in small:
        copy.wait()
    load_cot.wait()

    load_feat.wait()

    @pl.loop(0, slots)
    def _(b):
        ext_m[b] = feat[b, 48:64, :]
        ext_p[b] = feat[b, 0:16, :]

    pl.semaphore_wait(barrier, ns - 1 + nx - 1 + ny - 1)

    halo_right = remote(
        ext_m.at[pl.ds(0, slots)], ext_m.at[pl.ds(slots, slots)], halo_ss.at[0], halo_rs.at[0],
        space_peer(lax.rem(me + 1, ns)),
    )
    halo_left = remote(
        ext_p.at[pl.ds(0, slots)], ext_p.at[pl.ds(slots, slots)], halo_ss.at[1], halo_rs.at[1],
        space_peer(lax.rem(me + ns - 1, ns)),
    )
    halo_right.start()
    halo_left.start()

    def cot_copy(h, i, c):
        dest = lax.rem(z - offset(i) + nz, nz) * 2 + c
        return remote(outbuf.at[h, i, c], inbuf.at[h, i, core], cot_ss.at[h, i, c], cot_rs.at[h, i, core], space_peer(dest))

    def cot_arrival(h, i, e):
        return remote(outbuf.at[h, i, e], inbuf.at[h, i, e], cot_ss.at[h, i, e], cot_rs.at[h, i, e], sibling)

    def is_own(i, c):
        return (i == last) & (c == core)

    @pl.loop(0, ns)
    def _(t):
        i, c = t // 2, lax.rem(t, 2)
        dest = lax.rem(z - offset(i) + nz, nz) * 2 + c
        for place in range(2):
            wanted = dest * 2 + place
            pos = jnp.int32(0)
            for r in range(bal):
                pos = jnp.where(recv_s[0, r] == wanted, r, pos)
            block = cot[pos]
            for h in range(PARTS):
                outbuf[h, i, c, pl.ds(place * BV, BV), :] = block[:, h * LANES : (h + 1) * LANES]

        @pl.when(jnp.logical_not(is_own(i, c)))
        def _():
            cot_copy(0, i, c).start()

    inbuf[0, last, core] = outbuf[0, last, core]
    row = lax.broadcasted_iota(jnp.int32, (BV, channels), 0)
    by = lax.rem(row // 4, 4)
    bz = lax.rem(row, 4)
    keep = (by > 0, by < 3, bz > 0, bz < 3)
    own_shift = (4, 60, 1, 63)
    side_shift = (52, 12, 61, 3)

    @pl.loop(0, slots)
    def _(b):
        blk = feat[b]
        wide = blk.astype(F32)
        taps[b, :, 0:channels] = blk
        taps[b, 16:64, channels : 2 * channels] = blk[0:48]
        taps[b, 0:48, 2 * channels : 3 * channels] = blk[16:64]
        for k in range(4):
            n = jnp.minimum(nbr_s[2 + k, 0, b], slots)
            side = feat[n].astype(F32)
            tap = jnp.where(
                keep[k], pltpu.roll(wide, own_shift[k], 0), pltpu.roll(side, side_shift[k], 0)
            )
            taps[b, :, (3 + k) * channels : (4 + k) * channels] = tap.astype(BF16)

    halo_right.wait_recv()
    halo_left.wait_recv()

    @pl.loop(0, slots)
    def _(b):
        nm = jnp.minimum(nbr_s[0, 0, b], 2 * slots)
        np_ = nbr_s[1, 0, b]
        np_ = jnp.where(np_ < slots, np_, jnp.minimum(jnp.maximum(np_ - slots, slots), 2 * slots))
        taps[b, 0:16, channels : 2 * channels] = ext_m[nm]
        taps[b, 48:64, 2 * channels : 3 * channels] = ext_p[np_]

    @pl.loop(0, nz)
    def _(i):
        zs = lax.rem(z + offset(i), nz)
        for e in range(2):
            s = zs * 2 + e
            for k in range(7):
                cols = slice(k * channels, (k + 1) * channels)
                pair = jnp.concatenate(
                    [taps[send_s[0, 0, 0, s], :, cols], taps[send_s[0, 0, 1, s], :, cols]], 0
                )
                taps_t[i, cols, e * LANES : (e + 1) * LANES] = pair.T

    load_w.wait()
    live = counts_s[0, 0] * BV

    @pl.loop(0, slots // 4)
    def _(t):
        rows = taps[pl.ds(t * 4, 4)].reshape(4 * BV, taps_w)
        conv = jnp.dot(rows, w[...], preferred_element_type=F32)
        index = lax.broadcasted_iota(jnp.int32, (4 * BV, channels), 0) + t * (4 * BV)
        conv = jnp.where(index < live, conv, 0.0)
        vout[pl.ds(t * 4, 4)] = conv.astype(BF16).reshape(4, BV, channels)

    store_out = pltpu.make_async_copy(vout, out_hbm, local_sem.at[3])
    store_out.start()

    @pl.loop(0, ns)
    def _(t):
        i, c = t // 2, lax.rem(t, 2)

        @pl.when(jnp.logical_not(is_own(i, c)))
        def _():
            cot_copy(0, i, c).wait_send()
            cot_copy(1, i, c).start()

    inbuf[1, last, core] = outbuf[1, last, core]

    def await_places(h, first, end):
        for i in range(first, end):
            for e in range(2):
                if i == last:
                    @pl.when(e != core)
                    def _():
                        cot_arrival(h, i, e).wait_recv()
                else:
                    cot_arrival(h, i, e).wait_recv()

    def grad_places(h, first, end):
        await_places(h, first, end)
        for m in range(7):
            rows = slice(m * channels, (m + 1) * channels)
            acc[h, rows, :] = product(h, first, end, rows)

    def product(h, first, end, rows):
        term = None
        for i in range(first, end):
            part = jnp.dot(
                taps_t[i, rows, :], inbuf[h, i].reshape(2 * LANES, LANES), preferred_element_type=F32
            )
            term = part if term is None else term + part
        return term

    def ring(n):
        return sorted(range(1, n), key=lambda d: min(d, n - d))

    def core_copy(h, d):
        return remote(core_out.at[h, d], core_in.at[h, d], core_ss.at[h, d], core_rs.at[h, d], sibling)

    def x_copy(h, d):
        return remote(x_out.at[h, d], x_in.at[h, d], x_ss.at[h, d], x_rs.at[h, d], x_peer(d))

    def y_copy(h, d):
        return remote(y_out.at[h, d], y_in.at[h, d], y_ss.at[h, d], y_rs.at[h, d], y_peer(d))

    def z_copy(h, d):
        return remote(zbuf.at[h, z], zbuf.at[h, z], z_ss.at[h, d], z_rs.at[h, d], z_peer(d))

    def z_arrival(h, d):
        zs = lax.rem(z - d + nz, nz)
        return remote(zbuf.at[h, zs], zbuf.at[h, zs], z_ss.at[h, d], z_rs.at[h, d], z_peer(d))

    def y_rows(v):
        return pl.ds(pl.multiple_of(v * yr, 16), yr)

    whole = xr // yr

    def piece(v, u, rows=yr):
        return pl.ds(pl.multiple_of(core * half + v * xr + u * yr, 16), rows)

    def yg_copy(h, d):
        mine = cbuf.at[h, piece(x, y)]
        return remote(mine, mine, yg_ss.at[h, d], yg_rs.at[h, d], y_peer(d))

    def yg_arrival(h, d):
        theirs = cbuf.at[h, piece(x, lax.rem(y - d + ny, ny))]
        return remote(theirs, theirs, yg_ss.at[h, d], yg_rs.at[h, d], y_peer(d))

    def xg_copy(h, u, d):
        mine = cbuf.at[h, piece(x, u)]
        return remote(mine, mine, xg_ss.at[h, u, d], xg_rs.at[h, u, d], x_peer(d))

    def xg_arrival(h, u, d):
        theirs = cbuf.at[h, piece(lax.rem(x - d + nx, nx), u)]
        return remote(theirs, theirs, xg_ss.at[h, u, d], xg_rs.at[h, u, d], x_peer(d))

    def cg_copy(h, d):
        mine = cbuf.at[h, piece(lax.rem(x - d + nx, nx), 0, xr)]
        return remote(mine, mine, cg_ss.at[h, d], cg_rs.at[h, d], sibling)

    def cg_arrival(h, d):
        start = (1 - core) * half + lax.rem(x - d + nx, nx) * xr
        theirs = cbuf.at[h, pl.ds(pl.multiple_of(start, 16), xr)]
        return remote(theirs, theirs, cg_ss.at[h, d], cg_rs.at[h, d], sibling)

    def store_wg(h):
        return pltpu.make_async_copy(
            cbuf.at[h], wg_hbm.at[:, pl.ds(h * LANES, LANES)], local_sem.at[4 + h]
        )

    def settle_sums(h):
        for d in range(nx):
            core_copy(h, d).wait_send()
        for d in range(1, nx):
            x_copy(h, d).wait_send()
        for d in range(1, ny):
            y_copy(h, d).wait_send()
        for d in range(1, nz):
            z_copy(h, d).wait_send()

    def settle_gathers(h):
        for d in range(1, nx):
            @pl.loop(0, whole)
            def _(u):
                xg_copy(h, u, d).wait_send()
        for d in range(1, ny):
            @pl.when(y < whole)
            def _():
                yg_copy(h, d).wait_send()

    def settle_places():
        halo_right.wait_send()
        halo_left.wait_send()

        @pl.loop(0, ns)
        def _(t):
            i, c = t // 2, lax.rem(t, 2)

            @pl.when(jnp.logical_not(is_own(i, c)))
            def _():
                cot_copy(PARTS - 1, i, c).wait_send()

    def grad_x(h, first, begun):
        await_places(h, first, nz)
        order = ring(nx)[::-1] + [0]

        def rows_of(c, d):
            start = c * half + lax.rem(x + d, nx) * xr
            return pl.ds(pl.multiple_of(start, 16), xr)

        def total(c, d):
            term = product(h, first, nz, rows_of(c, d))
            return term + acc[h, rows_of(c, d), :] if begun else term

        for d in order:
            core_out[h, d] = total(1 - core, d).astype(BF16)
            core_copy(h, d).start()
        for d in order:
            term = total(core, d)
            core_copy(h, d).wait_recv()
            term += core_in[h, d].astype(F32)
            if d:
                x_out[h, d] = term.astype(BF16)
                x_copy(h, d).start()
            else:
                gx[h, 0:xr, :] = term

    def sum_y(h):
        total = gx[h, 0:xr, :]
        for d in ring(nx):
            x_copy(h, d).wait_recv()
            total += x_in[h, d].astype(F32)
        gx[h, 0:xr, :] = total
        if xr < ny * yr:
            gx[h, xr : ny * yr, :] = jnp.zeros((ny * yr - xr, LANES), F32)
        for d in ring(ny)[::-1]:
            y_out[h, d] = gx[h, y_rows(lax.rem(y + d, ny)), :].astype(BF16)
            y_copy(h, d).start()

    def sum_z(h):
        total = gx[h, y_rows(y), :]
        for d in ring(ny):
            y_copy(h, d).wait_recv()
            total += y_in[h, d].astype(F32)
        zbuf[h, z] = total.astype(BF16)
        for d in ring(nz)[::-1]:
            z_copy(h, d).start()

    def spread_y(h):
        for d in range(1, nz):
            z_arrival(h, d).wait_recv()
        total = zbuf[h, 0].astype(F32)
        for v in range(1, nz):
            total += zbuf[h, v].astype(F32)

        @pl.when(y < whole)
        def _():
            cbuf[h, piece(x, y), :] = (total * scale).astype(BF16)
            for d in ring(ny)[::-1]:
                yg_copy(h, d).start()
            for d in ring(nx)[::-1]:
                xg_copy(h, y, d).start()

    def spread_x(h):
        for d in ring(ny):
            u = lax.rem(y - d + ny, ny)

            @pl.when(u < whole)
            def _():
                yg_arrival(h, d).wait_recv()
                for v in ring(nx)[::-1]:
                    xg_copy(h, u, v).start()
        cg_copy(h, 0).start()

    def spread_core(h):
        for d in ring(nx):
            @pl.loop(0, whole)
            def _(u):
                xg_arrival(h, u, d).wait_recv()

            cg_copy(h, d).start()

    def finish(h):
        for d in [0] + ring(nx):
            cg_arrival(h, d).wait_recv()
        store_wg(h).start()

    grad_x(0, 0, False)
    sum_y(0)
    grad_places(1, 0, nz // 2)
    grad_x(1, nz // 2, True)
    sum_z(0)
    sum_y(1)
    spread_y(0)
    sum_z(1)
    spread_x(0)
    settle_places()
    settle_sums(0)
    spread_y(1)
    spread_core(0)
    spread_x(1)
    finish(0)
    settle_sums(1)
    settle_gathers(0)
    for d in range(nx):
        cg_copy(0, d).wait_send()
    spread_core(1)
    settle_gathers(1)
    finish(1)

    for d in range(nx):
        cg_copy(1, d).wait_send()
    for h in range(PARTS):
        store_wg(h).wait()
    store_out.wait()


def hand_over(out_in, wg_in, out, wg, out_mid, wg_mid, in_sem, out_sem):
    pairs = []
    for src, mid, dst in ((out_in, out_mid, out), (wg_in, wg_mid, wg)):
        step = src.shape[0] // 8
        for i in range(8):
            part = pl.ds(i * step, step)
            n = len(pairs)
            pairs.append(
                (
                    pltpu.make_async_copy(src.at[part], mid.at[part], in_sem.at[n]),
                    pltpu.make_async_copy(mid.at[part], dst.at[part], out_sem.at[n]),
                )
            )
    for load, _ in pairs:
        load.start()
    for load, store in pairs:
        load.wait()
        store.start()
    for _, store in pairs:
        store.wait()


def shards(dp_size, space_size, features, cotangent, weights, counts, neighbours, send_list, recv_list):
    slots, channels = features.shape[1], features.shape[-1]
    bal = cotangent.shape[1]
    ny = 1 << (dp_size.bit_length() // 2)
    nx = dp_size // ny
    nz = space_size // 2
    taps_w = 7 * channels
    half = taps_w // 2
    xr = half // nx
    yr = -(-xr // (16 * ny)) * 16
    scale = 1.0 / math.sqrt(dp_size * space_size * bal * BV)
    dma = pltpu.SemaphoreType.DMA
    vmem = pltpu.VMEM
    smem = pltpu.SMEM
    any_spec = pl.BlockSpec(memory_space=pl.ANY)
    macs = 2 * slots * BV * taps_w * channels
    voxel_out, weight_grad = pl.pallas_call(
        functools.partial(kernel, (nx, ny, nz, slots, bal, channels, scale)),
        out_shape=(
            jax.ShapeDtypeStruct((slots, BV, channels), BF16),
            jax.ShapeDtypeStruct((taps_w, channels), BF16),
        ),
        in_specs=[any_spec] * 3 + [pl.BlockSpec(memory_space=smem)] + [any_spec] * 3,
        out_specs=(any_spec, any_spec),
        scratch_shapes=[
            smem((6, 1, slots), jnp.int32),
            smem((1, 1, 2, space_size), jnp.int32),
            smem((1, bal), jnp.int32),
            vmem((bal, BV, channels), BF16),
            vmem((slots + 1, BV, channels), BF16),
            vmem((taps_w, channels), BF16),
            vmem((2 * slots + 1, 16, channels), BF16),
            vmem((2 * slots + 1, 16, channels), BF16),
            vmem((slots + 1, BV, taps_w), BF16),
            vmem((nz, taps_w, 2 * LANES), BF16),
            vmem((slots, BV, channels), BF16),
            vmem((PARTS, nz, 2, 2 * BV, LANES), BF16),
            vmem((PARTS, nz, 2, 2 * BV, LANES), BF16),
            vmem((PARTS, taps_w, LANES), F32),
            vmem((PARTS, nx, xr, LANES), BF16),
            vmem((PARTS, nx, xr, LANES), BF16),
            vmem((PARTS, nx, xr, LANES), BF16),
            vmem((PARTS, nx, xr, LANES), BF16),
            vmem((PARTS, ny * yr, LANES), F32),
            vmem((PARTS, ny, yr, LANES), BF16),
            vmem((PARTS, ny, yr, LANES), BF16),
            vmem((PARTS, nz, yr, LANES), BF16),
            vmem((PARTS, taps_w, LANES), BF16),
            dma((7 + PARTS,)),
            dma((2,)),
            dma((2,)),
            dma((PARTS, nz, 2)),
            dma((PARTS, nz, 2)),
            dma((PARTS, nx)),
            dma((PARTS, nx)),
            dma((PARTS, nx)),
            dma((PARTS, nx)),
            dma((PARTS, ny)),
            dma((PARTS, ny)),
            dma((PARTS, nz)),
            dma((PARTS, nz)),
            dma((PARTS, ny)),
            dma((PARTS, ny)),
            dma((PARTS, ny, nx)),
            dma((PARTS, ny, nx)),
            dma((PARTS, nx)),
            dma((PARTS, nx)),
        ],
        compiler_params=pltpu.CompilerParams(
            collective_id=0, has_side_effects=True, vmem_limit_bytes=60 * 1024 * 1024
        ),
        cost_estimate=pl.CostEstimate(flops=4 * macs, bytes_accessed=6 << 20, transcendentals=0),
    )(
        cotangent[0], features[0], weights.reshape(taps_w, channels),
        counts, neighbours.transpose(2, 0, 1), send_list.transpose(0, 1, 3, 2), recv_list,
    )
    voxel_out, weight_grad = pl.pallas_call(
        hand_over,
        out_shape=(
            jax.ShapeDtypeStruct(voxel_out.shape, BF16),
            jax.ShapeDtypeStruct(weight_grad.shape, BF16),
        ),
        in_specs=[any_spec] * 2,
        out_specs=(any_spec, any_spec),
        scratch_shapes=[
            vmem(voxel_out.shape, BF16),
            vmem(weight_grad.shape, BF16),
            dma((16,)),
            dma((16,)),
        ],
        compiler_params=pltpu.CompilerParams(vmem_limit_bytes=60 * 1024 * 1024),
    )(voxel_out, weight_grad)
    return voxel_out[None], weight_grad.reshape(7, channels, channels)


def solution(mesh):
    placed = (
        P("dp", "space", None, None),
        P("dp", "space", None, None),
        P(),
        P("dp", "space"),
        P("dp", "space", None),
        P("dp", "space", None, None),
        P("dp", "space"),
    )
    return jax.shard_map(
        functools.partial(shards, mesh.shape["dp"], mesh.shape["space"]),
        mesh=mesh,
        in_specs=placed,
        out_specs=(P("dp", "space", None, None), P()),
        check_vma=False,
    )
```
